32 devices in a mesh: lon: 4 (over y, x), lat: 8 (over z, core).
Axes of the slice: x: 2, y: 2, z: 4, core: 2. Of those that a mesh axis runs over, the one named last changes fastest.
Arguments:
- ocean_state: float32 [4, 10, 512, 1024], P(None, None, 'lat', 'lon'), may hold values from -4 to 4
- surface_height: float32 [512, 1024], P('lat', 'lon'), may hold values from -4 to 4
- zonal_transport: float32 [512, 1024], P('lat', 'lon'), may hold values from -4 to 4
- meridional_transport: float32 [512, 1024], P('lat', 'lon'), may hold values from -4 to 4
- land_mask: int32 [512, 1024], P('lat', 'lon'), may hold values 0 or 1
- levels: int32 [512, 1024], P('lat', 'lon'), may hold values from 1 to 10
Outputs:
- next_state: float32 [4, 10, 512, 1024], P(None, None, 'lat', 'lon')
- next_surface: float32 [512, 1024], P('lat', 'lon')
- next_zonal: float32 [512, 1024], P('lat', 'lon')
- next_meridional: float32 [512, 1024], P('lat', 'lon')
- streamfunction: float32 [512, 1024], P('lat', 'lon')
The draws below stay inside these ranges and needn't reach their ends.
Inputs may be any that keep to these rules, and one draw needn't show every extreme that they name: `land_mask`: 1 marks a sea surface cell, 0 land.
All inputs are finite; a program needn't handle non-finite values. No bound on the sum of `land_mask` on one device may be relied on, other than what follows from the above.
Results may differ from the reference program's by a relative error of at most 0.0003.
Values sent between devices are 32-bit elements; how exact they have to be, the bound alone decides.
A program may use at most 64 MiB of HBM per device.

```python
import math
import jax
import jax.numpy as jnp
from jax import lax

K = 10
NSUB = 10
NX = 1024
NY = 512


def plant(values, own_key, least, largest):
    shape = values.shape
    place = [jax.random.randint(jax.random.fold_in(own_key, axis), (), 0, shape[axis]) for axis in range(len(shape))]
    values = values.at[tuple(place)].set(least)
    longest = shape.index(max(shape))
    place[longest] = (place[longest] + 1) % shape[longest]
    return values.at[tuple(place)].set(largest)


def steps_of(stream_key, dims, split, smallest, largest):
    level = 1.0
    for dim, shards_of in split:
        draws = jax.random.uniform(jax.random.fold_in(jax.random.fold_in(stream_key, 6), dim), (shards_of,), jnp.float32, smallest / len(split), largest / len(split))
        level = level * jnp.repeat(jnp.exp(draws), dims[dim] // shards_of).reshape((-1,) + (1,) * (len(dims) - 1 - dim))
    return level


def centred(key, dims, width, bound, split=(), kind=jnp.bfloat16):
    array = width * jax.random.normal(key, dims, jnp.float32)
    if split:
        array = array * steps_of(key, dims, split, -0.22, 0.18)
    return jnp.clip(array, -bound, bound).astype(kind)


def setup_inputs(seed: int = 0) -> dict:
    streams_of = jax.random.split(jax.random.key(seed), 7)
    return {
        "ocean_state": centred(streams_of[0], (4, K, NY, NX), 0.5, 4.0, ((2, 8), (3, 4)), jnp.float32),
        "surface_height": centred(streams_of[1], (NY, NX), 0.5, 4.0, ((0, 8), (1, 4)), jnp.float32),
        "zonal_transport": centred(streams_of[2], (NY, NX), 0.5, 4.0, ((0, 8), (1, 4)), jnp.float32),
        "meridional_transport": centred(streams_of[3], (NY, NX), 0.5, 4.0, ((0, 8), (1, 4)), jnp.float32),
        "land_mask": plant((jax.random.randint(streams_of[4], (NY, NX), 0, 5) < 4).astype(jnp.int32), jax.random.fold_in(streams_of[4], 1), 0, 1),
        "levels": plant(jax.random.randint(streams_of[5], (NY, NX), 1, K + 1), jax.random.fold_in(streams_of[5], 1), 1, K).astype(jnp.int32),
    }


eta_rate = 0.5
wave_rate = 0.8
forcing_rate = 0.1
tracer_step = 0.2
momentum_step = 0.2
diffusivity = 0.1

def to_middle(in_field):
    return in_field[..., 1:-1, 1:-1]

def to_east(in_field):
    return in_field[..., 1:-1, 2:]

def to_west(in_field):
    return in_field[..., 1:-1, :-2]

def to_north(in_field):
    return in_field[..., 2:, 1:-1]

def to_south(in_field):
    return in_field[..., :-2, 1:-1]

def thicknesses(level_count):
    level_index = jnp.arange(level_count, dtype=jnp.float32)
    return (level_index + 1.0) / (level_count * (level_count + 1) / 2.0)

def level_core(level_ext, carry, fields, thick_k, index_k):
    above_sum, force_x, force_y, col_depth = carry
    temper, saline, zonal_flow, merid_flow = fields
    wet_cells = (index_k < level_ext).astype(jnp.float32)
    density = (0.8 * saline - 0.3 * temper - 0.04 * temper * temper) * wet_cells
    layer_weight = density * thick_k
    pressure = above_sum + 0.5 * layer_weight
    above_sum = above_sum + layer_weight
    col_depth = col_depth + wet_cells * thick_k
    wet_mid = to_middle(wet_cells)
    wet_east = wet_mid * to_east(wet_cells)
    wet_west = wet_mid * to_west(wet_cells)
    wet_north = wet_mid * to_north(wet_cells)
    wet_south = wet_mid * to_south(wet_cells)
    grad_x = (to_east(pressure) - to_middle(pressure)) * wet_east
    grad_y = (to_north(pressure) - to_middle(pressure)) * wet_north
    u_east = to_middle(zonal_flow)
    u_west = to_west(zonal_flow)
    v_north = to_middle(merid_flow)
    v_south = to_south(merid_flow)

    def advect(tracer):
        centre = to_middle(tracer)
        flux_east = wet_east * (jnp.maximum(u_east, 0.0) * centre + jnp.minimum(u_east, 0.0) * to_east(tracer))
        flux_west = wet_west * (jnp.maximum(u_west, 0.0) * to_west(tracer) + jnp.minimum(u_west, 0.0) * centre)
        flux_north = wet_north * (jnp.maximum(v_north, 0.0) * centre + jnp.minimum(v_north, 0.0) * to_north(tracer))
        flux_south = wet_south * (jnp.maximum(v_south, 0.0) * to_south(tracer) + jnp.minimum(v_south, 0.0) * centre)
        mixing = diffusivity * (wet_east * (to_east(tracer) - centre) - wet_west * (centre - to_west(tracer)) + wet_north * (to_north(tracer) - centre) - wet_south * (centre - to_south(tracer)))
        return wet_mid * (centre + tracer_step * (flux_west - flux_east + flux_south - flux_north + mixing))
    zonal_next = wet_east * (u_east - momentum_step * grad_x)
    merid_next = wet_north * (v_north - momentum_step * grad_y)
    new_carry = (above_sum, force_x + grad_x * thick_k, force_y + grad_y * thick_k, col_depth)
    return (new_carry, (advect(temper), advect(saline), zonal_next, merid_next))

def extend(in_field, fold_weight):
    wrapped = jnp.concatenate([in_field[..., -1:], in_field, in_field[..., :1]], axis=-1)
    folded = jnp.flip(wrapped[..., -1:, :], axis=-1) * fold_weight
    bottom_rim = jnp.zeros_like(wrapped[..., :1, :])
    return jnp.concatenate([bottom_rim, wrapped, folded], axis=-2)

def reference(ocean_state, surface_height, zonal_transport, meridional_transport, land_mask, levels):
    level_count = ocean_state.shape[1]
    thickness = thicknesses(level_count)
    level_index = jnp.arange(level_count, dtype=jnp.float32)
    level_field = (land_mask * levels).astype(jnp.float32)
    level_ext = extend(level_field, 1.0)

    def per_level(carry, slices):
        temper, saline, zonal_flow, merid_flow, thick_k, index_k = slices
        fields = (extend(temper, 1.0), extend(saline, 1.0), extend(zonal_flow, 0.0), extend(merid_flow, 0.0))
        return level_core(level_ext, carry, fields, thick_k, index_k)
    start = (jnp.zeros((NY + 2, NX + 2), jnp.float32), jnp.zeros((NY, NX), jnp.float32), jnp.zeros((NY, NX), jnp.float32), jnp.zeros((NY + 2, NX + 2), jnp.float32))
    carry, outputs = lax.scan(per_level, start, (ocean_state[0], ocean_state[1], ocean_state[2], ocean_state[3], thickness, level_index))
    above_sum, force_x, force_y, col_depth = carry
    next_state = jnp.stack(list(outputs))
    depth_east = jnp.minimum(to_middle(col_depth), to_east(col_depth))
    depth_north = jnp.minimum(to_middle(col_depth), to_north(col_depth))
    open_east = (depth_east > 0.0).astype(jnp.float32)
    open_north = (depth_north > 0.0).astype(jnp.float32)
    surface_wet = (level_field > 0.0).astype(jnp.float32)
    surface = surface_height
    zonal_now = zonal_transport
    merid_now = meridional_transport
    for sub_step in range(NSUB):
        transports = extend(jnp.stack([zonal_now, merid_now]), 0.0)
        divergence = zonal_now - to_west(transports[0]) + (merid_now - to_south(transports[1]))
        surface = surface_wet * (surface - eta_rate * divergence)
        surface_ext = extend(surface, 1.0)
        zonal_now = open_east * (zonal_now - wave_rate * depth_east * (to_east(surface_ext) - to_middle(surface_ext)) - forcing_rate * force_x)
        merid_now = open_north * (merid_now - wave_rate * depth_north * (to_north(surface_ext) - to_middle(surface_ext)) - forcing_rate * force_y)
    streamfunction = -jnp.cumsum(zonal_now, axis=0) / math.sqrt(NY)
    return (next_state, surface, zonal_now, merid_now, streamfunction)
```

```python
import functools
import math

import jax
import jax.numpy as jnp
from jax import lax
from jax.experimental import pallas as pl
from jax.experimental.pallas import tpu as pltpu
from jax.sharding import PartitionSpec as P

NSUB = 10
RIM = 16
CH = 16
LANES = 128
F32 = jnp.float32
MESH = pl.DeviceIdType.MESH


def iota(shape, dim):
    return lax.broadcasted_iota(jnp.int32, shape, dim)


def exact_dot(a, b):
    return jnp.dot(a, b, precision=lax.Precision.HIGHEST, preferred_element_type=F32)


def anti(size):
    return (iota((size, size), 0) + iota((size, size), 1) == size - 1).astype(F32)


def anti_blocks(size, block):
    a, b = iota((size, size), 0), iota((size, size), 1)
    same = (a // block) == (b // block)
    return (same & (a % block + b % block == block - 1)).astype(F32)


def remote(src, dst, send, recv, where):
    return pltpu.make_async_remote_copy(
        src_ref=src, dst_ref=dst, send_sem=send, recv_sem=recv, device_id=where, device_id_type=MESH
    )


def kernel(
    nlat, nlon, K, R, C,
    st_hbm, s_hbm, u_hbm, v_hbm, mask_hbm, lev_hbm,
    ns, os_ref, ou_ref, ov_ref, op_ref,
    ts, uv, pr, ml, w, le, ln, fw0, fs0,
    pcw, pce, re, rw, pkn, pks, rn, rs, fold1, fold4, foldf,
    c2w, c2e, r2e, r2w, ae, an, dd, gg, tot, totr,
    lsem, ssem, rsem, tssem, trsem,
):
    lat, lon = lax.axis_index("lat"), lax.axis_index("lon")
    east, west = lax.rem(lon + 1, nlon), lax.rem(lon + nlon - 1, nlon)
    up, down = lax.rem(lat + 1, nlat), lax.rem(lat + nlat - 1, nlat)
    is_top, is_low = lat == nlat - 1, lat == 0
    not_top, not_low = lat < nlat - 1, lat > 0
    turned = nlon - 1 - lon
    W = C + LANES
    c0, c1 = RIM, RIM + R
    last = C - LANES

    barrier = pltpu.get_barrier_semaphore()
    for d in range(1, nlon):
        pl.semaphore_signal(
            barrier, inc=1, device_id={"lon": lax.rem(lon + d, nlon)}, device_id_type=MESH
        )
    for d in range(1, nlat):
        pl.semaphore_signal(
            barrier, inc=1, device_id={"lat": lax.rem(lat + d, nlat)}, device_id_type=MESH
        )

    loads = [
        pltpu.make_async_copy(mask_hbm, ml.at[0], lsem.at[0]),
        pltpu.make_async_copy(lev_hbm, ml.at[1], lsem.at[1]),
        pltpu.make_async_copy(st_hbm.at[0:2], ts.at[:, :, 0:R, :], lsem.at[2]),
        pltpu.make_async_copy(st_hbm.at[2:4], uv, lsem.at[3]),
        pltpu.make_async_copy(s_hbm, w.at[0, c0:c1, 0:C], lsem.at[4]),
        pltpu.make_async_copy(u_hbm, w.at[1, c0:c1, 0:C], lsem.at[5]),
        pltpu.make_async_copy(v_hbm, w.at[2, c0:c1, 0:C], lsem.at[6]),
    ]
    for load in loads:
        load.start()

    col_w = remote(pcw, re, ssem.at[0], rsem.at[0], {"lon": west})
    col_e = remote(pce, rw, ssem.at[1], rsem.at[1], {"lon": east})
    row_n = remote(pkn, rs, ssem.at[2], rsem.at[2], {"lat": up})
    row_s = remote(pks, rn, ssem.at[3], rsem.at[3], {"lat": down})
    row_f = remote(fold1, rn, ssem.at[2], rsem.at[3], {"lon": turned})
    hi, lo = pl.ds(c1 - RIM, RIM), pl.ds(c0, RIM)
    above, below = pl.ds(c1, RIM), pl.ds(0, RIM)
    cols = pl.ds(0, C)
    four, two = pl.ds(0, 4), pl.ds(4, 2)
    wid_n = remote(w.at[four, hi, cols], w.at[four, below, cols], ssem.at[4], rsem.at[4], {"lat": up})
    wid_s = remote(w.at[four, lo, cols], w.at[four, above, cols], ssem.at[5], rsem.at[5], {"lat": down})
    wid_f = remote(fold4, w.at[four, above, cols], ssem.at[4], rsem.at[5], {"lon": turned})
    frc_n = remote(w.at[two, hi, cols], w.at[two, below, cols], ssem.at[6], rsem.at[6], {"lat": up})
    frc_s = remote(w.at[two, lo, cols], w.at[two, above, cols], ssem.at[7], rsem.at[7], {"lat": down})
    frc_f = remote(foldf, w.at[two, above, cols], ssem.at[6], rsem.at[7], {"lon": turned})
    far_w = remote(c2w, r2e, ssem.at[8], rsem.at[8], {"lon": west})
    far_e = remote(c2e, r2w, ssem.at[9], rsem.at[9], {"lon": east})

    @pl.when(is_low)
    def _():
        w[:, 0:RIM, 0:C] = jnp.zeros((6, RIM, C), F32)
        rs[...] = jnp.zeros(rs.shape, F32)

    dd[...] = jnp.zeros(dd.shape, F32)
    gg[...] = jnp.zeros(gg.shape, F32)

    lane = iota((CH, LANES), 1)
    lane_c = iota((CH, C), 1)
    row_c = iota((CH, C), 0)
    chunks = range(0, R, CH)
    loads[0].wait()
    loads[1].wait()
    for r in chunks:
        level = (ml[0, r : r + CH, :] * ml[1, r : r + CH, :]).astype(F32)
        w[3, c0 + r : c0 + r + CH, 0:C] = level
        l0, l1 = level[:, :LANES], level[:, last:]
        pcw[r : r + CH, :] = jnp.where(lane == 3 * K, pltpu.roll(l0, 3 * K, 1), 0.0)
        pce[r : r + CH, :] = jnp.where(lane == 3 * K, pltpu.roll(l1, 3 * K + 1, 1), 0.0)
    loads[2].wait()
    loads[3].wait()
    per = 2.0 / (K * (K + 1))

    def pressure_level(k, sums):
        kf = k.astype(F32)
        thick = (kf + 1.0) * per
        out = []
        for i, r in enumerate(chunks):
            rr = slice(r, r + CH)
            t, s = ts[0, k, rr, :], ts[1, k, rr, :]
            level = w[3, c0 + r : c0 + r + CH, 0:C]
            weight = jnp.where(kf < level, 0.8 * s - 0.3 * t - 0.04 * t * t, 0.0) * thick
            press = sums[i] + 0.5 * weight
            out.append(sums[i] + weight)
            pr[k, rr, :] = press
            u1 = uv[0, k, rr, last:]
            t0, s0, p0 = t[:, :LANES], s[:, :LANES], press[:, :LANES]
            t1, s1 = t[:, last:], s[:, last:]
            a = pcw[rr, :]
            a = jnp.where(lane == k, pltpu.roll(t0, k, 1), a)
            a = jnp.where(lane == K + k, pltpu.roll(s0, K + k, 1), a)
            a = jnp.where(lane == 2 * K + k, pltpu.roll(p0, 2 * K + k, 1), a)
            pcw[rr, :] = a
            b = pce[rr, :]
            b = jnp.where(lane == k, pltpu.roll(t1, k + 1, 1), b)
            b = jnp.where(lane == K + k, pltpu.roll(s1, K + k + 1, 1), b)
            b = jnp.where(lane == 2 * K + k, pltpu.roll(u1, 2 * K + k + 1, 1), b)
            pce[rr, :] = b
        return tuple(out)

    lax.fori_loop(0, K, pressure_level, tuple(jnp.zeros((CH, C), F32) for _ in chunks))
    for k in range(K):
        pkn[k : k + 1, :] = ts[0, k, R - 1 : R, :]
        pkn[K + k : K + k + 1, :] = ts[1, k, R - 1 : R, :]
        pkn[2 * K + k : 2 * K + k + 1, :] = uv[1, k, R - 1 : R, :]
        pks[k : k + 1, :] = ts[0, k, 0:1, :]
        pks[K + k : K + k + 1, :] = ts[1, k, 0:1, :]
        pks[2 * K + k : 2 * K + k + 1, :] = pr[k, 0:1, :]
    pkn[3 * K : 3 * K + 1, :] = w[3, c1 - 1 : c1, 0:C]
    pks[3 * K : 3 * K + 1, :] = w[3, c0 : c0 + 1, 0:C]

    pl.semaphore_wait(barrier, nlat + nlon - 2)

    @pl.when(is_top)
    def _():
        for k in range(K):
            fold1[k : k + 1, :] = ts[0, k, R - 1 : R, :]
            fold1[K + k : K + k + 1, :] = ts[1, k, R - 1 : R, :]
            fold1[2 * K + k : 2 * K + k + 1, :] = pr[k, R - 1 : R, :]
        fold1[3 * K : 3 * K + 1, :] = w[3, c1 - 1 : c1, 0:C]
        fold1[3 * K + 1 :, :] = jnp.zeros((fold1.shape[0] - 3 * K - 1, C), F32)
        fold1[...] = exact_dot(fold1[...], anti(C))
        row_f.start()

    col_w.start()
    col_e.start()

    @pl.when(not_top)
    def _():
        row_n.start()

    @pl.when(not_low)
    def _():
        row_s.start()

    for load in loads[4:]:
        load.wait()

    @pl.when(not_top)
    def _():
        wid_n.start()

    @pl.when(is_top)
    def _():
        rows4 = jnp.concatenate([w[f, c1 - RIM : c1, 0:C] for f in range(4)], axis=0)
        flipped = exact_dot(exact_dot(anti_blocks(4 * RIM, RIM), rows4), anti(C))
        for f in range(4):
            fold4[f] = flipped[f * RIM : (f + 1) * RIM]
        wid_f.start()

    @pl.when(not_low)
    def _():
        wid_s.start()

    col_w.wait_recv()
    row_s.wait_recv()
    for k in range(K):
        ts[0, k, R : R + 1, :] = rn[k : k + 1, :]
        ts[1, k, R : R + 1, :] = rn[K + k : K + k + 1, :]
        pr[k, R : R + 1, :] = rn[2 * K + k : 2 * K + k + 1, :]

    def eastward(centre, rim, shift):
        rolled = pltpu.roll(centre, C - 1, 1)
        h = pltpu.roll(rim, shift, 1)
        edge = jnp.where(lane == LANES - 1, h, rolled[:, last:])
        return jnp.concatenate([rolled[:, :last], edge], axis=1)

    for r in chunks:
        level = w[3, c0 + r : c0 + r + CH, 0:C]
        le[r : r + CH, :] = jnp.minimum(
            level, eastward(level, re[r : r + CH, :], LANES - 1 - 3 * K)
        )
        if r + CH < R:
            north = w[3, c0 + r + 1 : c0 + r + CH + 1, 0:C]
        else:
            north = jnp.where(
                row_c == CH - 1, rn[3 * K : 3 * K + 1, :], pltpu.roll(level, CH - 1, 0)
            )
        ln[r : r + CH, :] = jnp.minimum(level, north)

    for r in chunks:
        rr = slice(r, r + CH)
        le_r, ln_r, rim = le[rr, :], ln[rr, :], re[rr, :]

        def force_level(k, sums):
            fx, fy = sums
            kf = k.astype(F32)
            thick = (kf + 1.0) * per
            press = pr[k, rr, :]
            p_e = eastward(press, rim, LANES - 1 - 2 * K - k)
            p_n = pr[k, r + 1 : r + CH + 1, :]
            open_e, open_n = kf < le_r, kf < ln_r
            gx = jnp.where(open_e, p_e - press, 0.0)
            gy = jnp.where(open_n, p_n - press, 0.0)
            ns[2, k, rr, :] = jnp.where(open_e, uv[0, k, rr, :] - 0.2 * gx, 0.0)
            ns[3, k, rr, :] = jnp.where(open_n, uv[1, k, rr, :] - 0.2 * gy, 0.0)
            return fx + gx * thick, fy + gy * thick

        zero = jnp.zeros((CH, C), F32)
        fx, fy = lax.fori_loop(0, K, force_level, (zero, zero))
        w[4, c0 + r : c0 + r + CH, 0:C] = 0.1 * fx
        w[5, c0 + r : c0 + r + CH, 0:C] = 0.1 * fy

    @pl.when(not_top)
    def _():
        frc_n.start()

    @pl.when(is_top)
    def _():
        rows2 = jnp.concatenate([w[f, c1 - RIM : c1, 0:C] for f in (4, 5)], axis=0)
        flipped = exact_dot(exact_dot(anti_blocks(2 * RIM, RIM), rows2), anti(C))
        foldf[0] = flipped[:RIM]
        foldf[1] = flipped[RIM:]
        frc_f.start()

    @pl.when(not_low)
    def _():
        frc_s.start()

    col_e.wait_recv()

    @pl.when(not_low)
    def _():
        row_n.wait_recv()

    lane_f = jnp.where(lane < K, lane, lane - K).astype(F32)
    for r in chunks:
        rr = slice(r, r + CH)
        a, b = rw[rr, :], pcw[rr, :]
        u = jnp.where(lane < K, pltpu.roll(a, LANES - 2 * K, 1), pltpu.roll(a, LANES - K, 1))
        shallow = jnp.minimum(a[:, 3 * K : 3 * K + 1], b[:, 3 * K : 3 * K + 1])
        flux = (jnp.maximum(u, 0.0) + 0.1) * a + (jnp.minimum(u, 0.0) - 0.1) * b
        fw0[rr, :] = jnp.where(lane_f < shallow, flux, 0.0)
    row_k = iota((K, C), 0).astype(F32)
    shallow = jnp.minimum(rs[3 * K : 3 * K + 1, :], pks[3 * K : 3 * K + 1, :])
    v_rim = rs[2 * K : 3 * K, :]
    vp, vm = jnp.maximum(v_rim, 0.0) + 0.1, jnp.minimum(v_rim, 0.0) - 0.1
    for q in range(2):
        flux = vp * rs[q * K : (q + 1) * K, :] + vm * pks[q * K : (q + 1) * K, :]
        flux = jnp.where(row_k < shallow, flux, 0.0)
        for k in range(K):
            fs0[q, k] = flux[k : k + 1, :]

    def tracer_level(k, carry):
        kf = k.astype(F32)
        south_row = [fs0[q, k] for q in range(2)]
        for r in chunks:
            rr = slice(r, r + CH)
            u, v = uv[0, k, rr, :], uv[1, k, rr, :]
            u_p, u_m = jnp.maximum(u, 0.0) + 0.1, jnp.minimum(u, 0.0) - 0.1
            v_p, v_m = jnp.maximum(v, 0.0) + 0.1, jnp.minimum(v, 0.0) - 0.1
            wet = kf < w[3, c0 + r : c0 + r + CH, 0:C]
            wet_e, wet_n = kf < le[rr, :], kf < ln[rr, :]
            rim_e, rim_w = re[rr, :], fw0[rr, :]
            for q in range(2):
                c = ts[q, k, rr, :]
                fe = jnp.where(
                    wet_e, u_p * c + u_m * eastward(c, rim_e, LANES - 1 - q * K - k), 0.0
                )
                fn = jnp.where(wet_n, v_p * c + v_m * ts[q, k, r + 1 : r + CH + 1, :], 0.0)
                h = pltpu.roll(rim_w, LANES - q * K - k if q else lax.rem(LANES - k, LANES), 1)
                rolled = pltpu.roll(fe, 1, 1)
                fw = jnp.concatenate(
                    [jnp.where(lane == 0, h, rolled[:, :LANES]), rolled[:, LANES:]], axis=1
                )
                fs = jnp.where(row_c == 0, south_row[q], pltpu.roll(fn, 1, 0))
                south_row[q] = fn[CH - 1 : CH, :]
                ns[q, k, rr, :] = jnp.where(wet, c + 0.2 * (fw - fe + fs - fn), 0.0)
        return carry

    first, second = (4 * K) // 10, (8 * K) // 10
    lax.fori_loop(0, first, tracer_level, 0)

    wid_s.wait_recv()
    frc_s.wait_recv()

    @pl.when(not_low)
    def _():
        wid_n.wait_recv()
        frc_n.wait_recv()

    wide_rows = range(0, R + 2 * RIM, CH)
    for r in wide_rows:
        a = jnp.zeros((CH, LANES), F32)
        b = jnp.zeros((CH, LANES), F32)
        for f in range(6):
            mine = (lane >= f * RIM) & (lane < (f + 1) * RIM)
            x0 = w[f, r : r + CH, 0:LANES]
            x1 = w[f, r : r + CH, last:C]
            a = jnp.where(mine, pltpu.roll(x0, f * RIM, 1) if f else x0, a)
            b = jnp.where(mine, pltpu.roll(x1, (RIM + f * RIM) % LANES, 1), b)
        c2w[r : r + CH, :] = a
        c2e[r : r + CH, :] = b
    far_w.start()
    far_e.start()
    lax.fori_loop(first, second, tracer_level, 0)
    far_w.wait_recv()
    far_e.wait_recv()
    for r in wide_rows:
        a, b = r2e[r : r + CH, :], r2w[r : r + CH, :]
        for f in range(6):
            x = pltpu.roll(a, LANES - f * RIM, 1) if f else a
            y = pltpu.roll(b, (LANES - RIM - f * RIM) % LANES, 1)
            w[f, r : r + CH, C:W] = jnp.where(
                lane < RIM, x, jnp.where(lane >= LANES - RIM, y, 0.0)
            )

    @pl.when(not_top)
    def _():
        row_n.wait_send()
        wid_n.wait_send()
        frc_n.wait_send()

    @pl.when(not_low)
    def _():
        row_s.wait_send()
        wid_s.wait_send()
        frc_s.wait_send()

    lane_w = iota((CH, W), 1)
    row_w = iota((CH, W), 0)

    @pl.when(is_top)
    def _():
        row_f.wait_send()
        wid_f.wait_send()
        frc_f.wait_send()
        fold = slice(c1, c1 + RIM)
        for f in (1, 4):
            w[f, fold, :] = -pltpu.roll(w[f, fold, :], W - 1, 1)
        for f, where in ((2, dd), (5, gg)):
            x = w[f, fold, :]
            where[...] = jnp.where(row_w == 0, w[f, c1 - 1 : c1, :] + x, 0.0)
            w[f, fold, :] = -pltpu.roll(x, RIM - 1, 0)

    def wide_depth(shallow):
        return (shallow * (shallow + 1.0)) * (0.8 / (K * (K + 1)))

    def shifted_rows(ref, f, r, by):
        low = r + by
        if low < 0 or low + CH > R + 2 * RIM:
            return pltpu.roll(ref[f, r : r + CH, :], (-by) % CH, 0)
        return ref[f, low : low + CH, :]

    def surface_step(first_step):
        for r in wide_rows:
            rr = slice(r, r + CH)
            u, v = w[1, rr, :], w[2, rr, :]
            div = u - pltpu.roll(u, 1, 1) + (v - shifted_rows(w, 2, r, -1))
            if r == c1:
                div = div + dd[...]
            new = w[0, rr, :] - 0.5 * div
            if first_step:
                new = jnp.where(w[3, rr, :] > 0.0, new, 0.0)
            w[0, rr, :] = new

    def transport_step(first_step):
        for r in wide_rows:
            rr = slice(r, r + CH)
            s, u, v = w[0, rr, :], w[1, rr, :], w[2, rr, :]
            if first_step:
                level = w[3, rr, :]
                shallow_e = jnp.minimum(level, pltpu.roll(level, W - 1, 1))
                shallow_n = jnp.minimum(level, shifted_rows(w, 3, r, 1))
                ae[rr, :] = wide_depth(shallow_e)
                an[rr, :] = wide_depth(shallow_n)
                u = jnp.where(shallow_e > 0.0, u, 0.0)
                v = jnp.where(shallow_n > 0.0, v, 0.0)
            w[1, rr, :] = u - ae[rr, :] * (pltpu.roll(s, W - 1, 1) - s) - w[4, rr, :]
            w[2, rr, :] = v - an[rr, :] * (shifted_rows(w, 0, r, 1) - s) - w[5, rr, :]

    surface_step(True)
    transport_step(True)
    dd[...] = jnp.where(an[c1 - 1 : c1, :] > 0.0, dd[...], 0.0) - gg[...]

    def substep(i, carry):
        surface_step(False)
        transport_step(False)
        dd[...] = dd[...] - gg[...]
        return carry

    lax.fori_loop(1, NSUB, substep, 0)

    low_tri = (iota((R, R), 0) >= iota((R, R), 1)).astype(F32)
    zonal = w[1, c0:c1, 0:C]
    op_ref[...] = exact_dot(low_tri, zonal)
    tot[...] = jnp.broadcast_to(op_ref[R - 1 : R, :], tot.shape)
    sends = []
    for d in range(1, nlat):
        sends.append(
            remote(
                tot, totr.at[d - 1], tssem.at[d - 1], trsem.at[d - 1],
                {"lat": lax.rem(lat + d, nlat)},
            )
        )
    for send in sends:
        send.start()
    lax.fori_loop(second, K, tracer_level, 0)
    os_ref[...] = w[0, c0:c1, 0:C]
    ou_ref[...] = zonal
    ov_ref[...] = w[2, c0:c1, 0:C]
    south = jnp.zeros((8, C), F32)
    for d in range(1, nlat):
        sends[d - 1].wait_recv()
        south = south + totr[d - 1] * (lat >= d).astype(F32)
    scale = -1.0 / math.sqrt(R * nlat)
    op_ref[...] = (op_ref[...] + south[0:1, :]) * scale
    for send in sends:
        send.wait_send()
    for copy in (col_w, col_e, far_w, far_e):
        copy.wait_send()


def body(ocean_state, surface_height, zonal_transport, meridional_transport, land_mask, levels):
    nlat, nlon = lax.axis_size("lat"), lax.axis_size("lon")
    _, K, R, C = ocean_state.shape
    wide = (R + 2 * RIM, C + LANES)
    plane = jax.ShapeDtypeStruct((R, C), F32)
    pack = -(-(3 * K + 1) // 8) * 8
    vm = lambda *shape: pltpu.VMEM(shape, F32)
    dma = lambda n: pltpu.SemaphoreType.DMA((n,))
    return pl.pallas_call(
        functools.partial(kernel, nlat, nlon, K, R, C),
        out_shape=(jax.ShapeDtypeStruct(ocean_state.shape, F32), plane, plane, plane, plane),
        in_specs=[pl.BlockSpec(memory_space=pltpu.HBM)] * 6,
        out_specs=(pl.BlockSpec(memory_space=pltpu.VMEM),) * 5,
        scratch_shapes=[
            vm(2, K, R + 8, C), vm(2, K, R, C), vm(K, R + 8, C),
            pltpu.VMEM((2, R, C), jnp.int32),
            vm(6, *wide), vm(R, C), vm(R, C), vm(R, LANES), vm(2, K, 1, C),
            vm(R, LANES), vm(R, LANES), vm(R, LANES), vm(R, LANES),
            vm(pack, C), vm(pack, C), vm(pack, C), vm(pack, C), vm(pack, C),
            vm(4, RIM, C), vm(2, RIM, C),
            vm(wide[0], LANES), vm(wide[0], LANES), vm(wide[0], LANES), vm(wide[0], LANES),
            vm(*wide), vm(*wide), vm(RIM, wide[1]), vm(RIM, wide[1]),
            vm(8, C), vm(nlat - 1, 8, C),
            dma(7), dma(10), dma(10), dma(nlat - 1), dma(nlat - 1),
        ],
        compiler_params=pltpu.CompilerParams(
            collective_id=0, has_side_effects=True, vmem_limit_bytes=40 * 1024 * 1024
        ),
        cost_estimate=pl.CostEstimate(
            flops=40_000_000, bytes_accessed=2 * ocean_state.size * 4, transcendentals=0
        ),
    )(ocean_state, surface_height, zonal_transport, meridional_transport, land_mask, levels)


def solution(mesh):
    cells = P("lat", "lon")
    full = P(None, None, "lat", "lon")
    return jax.shard_map(
        body,
        mesh=mesh,
        in_specs=(full, cells, cells, cells, cells, cells),
        out_specs=(full, cells, cells, cells, cells),
        check_vma=False,
    )
```

```python
import functools
import math

import jax
import jax.numpy as jnp
from jax import lax
from jax.experimental import pallas as pl
from jax.experimental.pallas import tpu as pltpu
from jax.sharding import PartitionSpec as P

NSUB = 10
RIM = 16
CH = 16
LANES = 128
F32 = jnp.float32
MESH = pl.DeviceIdType.MESH


def iota(shape, dim):
    return lax.broadcasted_iota(jnp.int32, shape, dim)


def exact_dot(a, b):
    return jnp.dot(a, b, precision=lax.Precision.HIGHEST, preferred_element_type=F32)


def anti(size):
    return (iota((size, size), 0) + iota((size, size), 1) == size - 1).astype(F32)


def anti_blocks(size, block):
    a, b = iota((size, size), 0), iota((size, size), 1)
    same = (a // block) == (b // block)
    return (same & (a % block + b % block == block - 1)).astype(F32)


def remote(src, dst, send, recv, where):
    return pltpu.make_async_remote_copy(
        src_ref=src, dst_ref=dst, send_sem=send, recv_sem=recv, device_id=where, device_id_type=MESH
    )


def kernel(
    nlat, nlon, K, R, C,
    st_hbm, s_hbm, u_hbm, v_hbm, mask_hbm, lev_hbm,
    ns, os_ref, ou_ref, ov_ref, op_ref,
    ts, uv, pr, ml, w, le, ln, fw0, fs0,
    pcw, pce, re, rw, pkn, pks, rn, rs, fold1, fold4, foldf,
    c2w, c2e, r2e, r2w, ae, an, dd, gg, tot, totr,
    lsem, ssem, rsem, tssem, trsem,
):
    lat, lon = lax.axis_index("lat"), lax.axis_index("lon")
    east, west = lax.rem(lon + 1, nlon), lax.rem(lon + nlon - 1, nlon)
    up, down = lax.rem(lat + 1, nlat), lax.rem(lat + nlat - 1, nlat)
    is_top, is_low = lat == nlat - 1, lat == 0
    not_top, not_low = lat < nlat - 1, lat > 0
    turned = nlon - 1 - lon
    W = C + LANES
    c0, c1 = RIM, RIM + R
    last = C - LANES

    barrier = pltpu.get_barrier_semaphore()
    for d in range(1, nlon):
        pl.semaphore_signal(
            barrier, inc=1, device_id={"lon": lax.rem(lon + d, nlon)}, device_id_type=MESH
        )
    for d in range(1, nlat):
        pl.semaphore_signal(
            barrier, inc=1, device_id={"lat": lax.rem(lat + d, nlat)}, device_id_type=MESH
        )

    loads = [
        pltpu.make_async_copy(mask_hbm, ml.at[0], lsem.at[0]),
        pltpu.make_async_copy(lev_hbm, ml.at[1], lsem.at[1]),
        pltpu.make_async_copy(st_hbm.at[0:2], ts.at[:, :, 0:R, :], lsem.at[2]),
        pltpu.make_async_copy(st_hbm.at[2:4], uv, lsem.at[3]),
        pltpu.make_async_copy(s_hbm, w.at[0, c0:c1, 0:C], lsem.at[4]),
        pltpu.make_async_copy(u_hbm, w.at[1, c0:c1, 0:C], lsem.at[5]),
        pltpu.make_async_copy(v_hbm, w.at[2, c0:c1, 0:C], lsem.at[6]),
    ]
    for load in loads:
        load.start()

    col_w = remote(pcw, re, ssem.at[0], rsem.at[0], {"lon": west})
    col_e = remote(pce, rw, ssem.at[1], rsem.at[1], {"lon": east})
    row_n = remote(pkn, rs, ssem.at[2], rsem.at[2], {"lat": up})
    row_s = remote(pks, rn, ssem.at[3], rsem.at[3], {"lat": down})
    row_f = remote(fold1, rn, ssem.at[2], rsem.at[3], {"lon": turned})
    hi, lo = pl.ds(c1 - RIM, RIM), pl.ds(c0, RIM)
    above, below = pl.ds(c1, RIM), pl.ds(0, RIM)
    cols = pl.ds(0, C)
    four, two = pl.ds(0, 4), pl.ds(4, 2)
    wid_n = remote(w.at[four, hi, cols], w.at[four, below, cols], ssem.at[4], rsem.at[4], {"lat": up})
    wid_s = remote(w.at[four, lo, cols], w.at[four, above, cols], ssem.at[5], rsem.at[5], {"lat": down})
    wid_f = remote(fold4, w.at[four, above, cols], ssem.at[4], rsem.at[5], {"lon": turned})
    frc_n = remote(w.at[two, hi, cols], w.at[two, below, cols], ssem.at[6], rsem.at[6], {"lat": up})
    frc_s = remote(w.at[two, lo, cols], w.at[two, above, cols], ssem.at[7], rsem.at[7], {"lat": down})
    frc_f = remote(foldf, w.at[two, above, cols], ssem.at[6], rsem.at[7], {"lon": turned})
    far_w = remote(c2w, r2e, ssem.at[8], rsem.at[8], {"lon": west})
    far_e = remote(c2e, r2w, ssem.at[9], rsem.at[9], {"lon": east})

    @pl.when(is_low)
    def _():
        w[:, 0:RIM, 0:C] = jnp.zeros((6, RIM, C), F32)
        rs[...] = jnp.zeros(rs.shape, F32)

    dd[...] = jnp.zeros(dd.shape, F32)
    gg[...] = jnp.zeros(gg.shape, F32)

    lane = iota((CH, LANES), 1)
    lane_c = iota((CH, C), 1)
    row_c = iota((CH, C), 0)
    chunks = range(0, R, CH)
    loads[0].wait()
    loads[1].wait()
    for r in chunks:
        level = (ml[0, r : r + CH, :] * ml[1, r : r + CH, :]).astype(F32)
        w[3, c0 + r : c0 + r + CH, 0:C] = level
        l0, l1 = level[:, :LANES], level[:, last:]
        pcw[r : r + CH, :] = jnp.where(lane == 3 * K, pltpu.roll(l0, 3 * K, 1), 0.0)
        pce[r : r + CH, :] = jnp.where(lane == 3 * K, pltpu.roll(l1, 3 * K + 1, 1), 0.0)
    loads[2].wait()
    loads[3].wait()
    per = 2.0 / (K * (K + 1))

    def pressure_level(k, sums):
        kf = k.astype(F32)
        thick = (kf + 1.0) * per
        out = []
        for i, r in enumerate(chunks):
            rr = slice(r, r + CH)
            t, s = ts[0, k, rr, :], ts[1, k, rr, :]
            level = w[3, c0 + r : c0 + r + CH, 0:C]
            weight = jnp.where(kf < level, 0.8 * s - 0.3 * t - 0.04 * t * t, 0.0) * thick
            press = sums[i] + 0.5 * weight
            out.append(sums[i] + weight)
            pr[k, rr, :] = press
            u1 = uv[0, k, rr, last:]
            t0, s0, p0 = t[:, :LANES], s[:, :LANES], press[:, :LANES]
            t1, s1 = t[:, last:], s[:, last:]
            a = pcw[rr, :]
            a = jnp.where(lane == k, pltpu.roll(t0, k, 1), a)
            a = jnp.where(lane == K + k, pltpu.roll(s0, K + k, 1), a)
            a = jnp.where(lane == 2 * K + k, pltpu.roll(p0, 2 * K + k, 1), a)
            pcw[rr, :] = a
            b = pce[rr, :]
            b = jnp.where(lane == k, pltpu.roll(t1, k + 1, 1), b)
            b = jnp.where(lane == K + k, pltpu.roll(s1, K + k + 1, 1), b)
            b = jnp.where(lane == 2 * K + k, pltpu.roll(u1, 2 * K + k + 1, 1), b)
            pce[rr, :] = b
        return tuple(out)

    lax.fori_loop(0, K, pressure_level, tuple(jnp.zeros((CH, C), F32) for _ in chunks))
    for k in range(K):
        pkn[k : k + 1, :] = ts[0, k, R - 1 : R, :]
        pkn[K + k : K + k + 1, :] = ts[1, k, R - 1 : R, :]
        pkn[2 * K + k : 2 * K + k + 1, :] = uv[1, k, R - 1 : R, :]
        pks[k : k + 1, :] = ts[0, k, 0:1, :]
        pks[K + k : K + k + 1, :] = ts[1, k, 0:1, :]
        pks[2 * K + k : 2 * K + k + 1, :] = pr[k, 0:1, :]
    pkn[3 * K : 3 * K + 1, :] = w[3, c1 - 1 : c1, 0:C]
    pks[3 * K : 3 * K + 1, :] = w[3, c0 : c0 + 1, 0:C]

    pl.semaphore_wait(barrier, nlat + nlon - 2)

    @pl.when(is_top)
    def _():
        for k in range(K):
            fold1[k : k + 1, :] = ts[0, k, R - 1 : R, :]
            fold1[K + k : K + k + 1, :] = ts[1, k, R - 1 : R, :]
            fold1[2 * K + k : 2 * K + k + 1, :] = pr[k, R - 1 : R, :]
        fold1[3 * K : 3 * K + 1, :] = w[3, c1 - 1 : c1, 0:C]
        fold1[3 * K + 1 :, :] = jnp.zeros((fold1.shape[0] - 3 * K - 1, C), F32)
        fold1[...] = exact_dot(fold1[...], anti(C))
        row_f.start()

    col_w.start()
    col_e.start()

    @pl.when(not_top)
    def _():
        row_n.start()

    @pl.when(not_low)
    def _():
        row_s.start()

    for load in loads[4:]:
        load.wait()

    @pl.when(not_top)
    def _():
        wid_n.start()

    @pl.when(is_top)
    def _():
        rows4 = jnp.concatenate([w[f, c1 - RIM : c1, 0:C] for f in range(4)], axis=0)
        flipped = exact_dot(exact_dot(anti_blocks(4 * RIM, RIM), rows4), anti(C))
        for f in range(4):
            fold4[f] = flipped[f * RIM : (f + 1) * RIM]
        wid_f.start()

    @pl.when(not_low)
    def _():
        wid_s.start()

    col_w.wait_recv()
    row_s.wait_recv()
    for k in range(K):
        ts[0, k, R : R + 1, :] = rn[k : k + 1, :]
        ts[1, k, R : R + 1, :] = rn[K + k : K + k + 1, :]
        pr[k, R : R + 1, :] = rn[2 * K + k : 2 * K + k + 1, :]

    def eastward(centre, rim, shift):
        rolled = pltpu.roll(centre, C - 1, 1)
        h = pltpu.roll(rim, shift, 1)
        edge = jnp.where(lane == LANES - 1, h, rolled[:, last:])
        return jnp.concatenate([rolled[:, :last], edge], axis=1)

    for r in chunks:
        level = w[3, c0 + r : c0 + r + CH, 0:C]
        le[r : r + CH, :] = jnp.minimum(
            level, eastward(level, re[r : r + CH, :], LANES - 1 - 3 * K)
        )
        if r + CH < R:
            north = w[3, c0 + r + 1 : c0 + r + CH + 1, 0:C]
        else:
            north = jnp.where(
                row_c == CH - 1, rn[3 * K : 3 * K + 1, :], pltpu.roll(level, CH - 1, 0)
            )
        ln[r : r + CH, :] = jnp.minimum(level, north)

    for r in chunks:
        rr = slice(r, r + CH)
        le_r, ln_r, rim = le[rr, :], ln[rr, :], re[rr, :]

        def force_level(k, sums):
            fx, fy = sums
            kf = k.astype(F32)
            thick = (kf + 1.0) * per
            press = pr[k, rr, :]
            p_e = eastward(press, rim, LANES - 1 - 2 * K - k)
            p_n = pr[k, r + 1 : r + CH + 1, :]
            open_e, open_n = kf < le_r, kf < ln_r
            gx = jnp.where(open_e, p_e - press, 0.0)
            gy = jnp.where(open_n, p_n - press, 0.0)
            ns[2, k, rr, :] = jnp.where(open_e, uv[0, k, rr, :] - 0.2 * gx, 0.0)
            ns[3, k, rr, :] = jnp.where(open_n, uv[1, k, rr, :] - 0.2 * gy, 0.0)
            return fx + gx * thick, fy + gy * thick

        zero = jnp.zeros((CH, C), F32)
        fx, fy = lax.fori_loop(0, K, force_level, (zero, zero))
        w[4, c0 + r : c0 + r + CH, 0:C] = 0.1 * fx
        w[5, c0 + r : c0 + r + CH, 0:C] = 0.1 * fy

    @pl.when(not_top)
    def _():
        frc_n.start()

    @pl.when(is_top)
    def _():
        rows2 = jnp.concatenate([w[f, c1 - RIM : c1, 0:C] for f in (4, 5)], axis=0)
        flipped = exact_dot(exact_dot(anti_blocks(2 * RIM, RIM), rows2), anti(C))
        foldf[0] = flipped[:RIM]
        foldf[1] = flipped[RIM:]
        frc_f.start()

    @pl.when(not_low)
    def _():
        frc_s.start()

    col_e.wait_recv()

    @pl.when(not_low)
    def _():
        row_n.wait_recv()

    lane_f = jnp.where(lane < K, lane, lane - K).astype(F32)
    for r in chunks:
        rr = slice(r, r + CH)
        a, b = rw[rr, :], pcw[rr, :]
        u = jnp.where(lane < K, pltpu.roll(a, LANES - 2 * K, 1), pltpu.roll(a, LANES - K, 1))
        shallow = jnp.minimum(a[:, 3 * K : 3 * K + 1], b[:, 3 * K : 3 * K + 1])
        flux = (jnp.maximum(u, 0.0) + 0.1) * a + (jnp.minimum(u, 0.0) - 0.1) * b
        fw0[rr, :] = jnp.where(lane_f < shallow, flux, 0.0)
    row_k = iota((K, C), 0).astype(F32)
    shallow = jnp.minimum(rs[3 * K : 3 * K + 1, :], pks[3 * K : 3 * K + 1, :])
    v_rim = rs[2 * K : 3 * K, :]
    vp, vm = jnp.maximum(v_rim, 0.0) + 0.1, jnp.minimum(v_rim, 0.0) - 0.1
    for q in range(2):
        flux = vp * rs[q * K : (q + 1) * K, :] + vm * pks[q * K : (q + 1) * K, :]
        flux = jnp.where(row_k < shallow, flux, 0.0)
        for k in range(K):
            fs0[q, k] = flux[k : k + 1, :]

    def tracer_level(k, carry):
        kf = k.astype(F32)
        south_row = [fs0[q, k] for q in range(2)]
        for r in chunks:
            rr = slice(r, r + CH)
            u, v = uv[0, k, rr, :], uv[1, k, rr, :]
            u_p, u_m = jnp.maximum(u, 0.0) + 0.1, jnp.minimum(u, 0.0) - 0.1
            v_p, v_m = jnp.maximum(v, 0.0) + 0.1, jnp.minimum(v, 0.0) - 0.1
            wet = kf < w[3, c0 + r : c0 + r + CH, 0:C]
            wet_e, wet_n = kf < le[rr, :], kf < ln[rr, :]
            rim_e, rim_w = re[rr, :], fw0[rr, :]
            for q in range(2):
                c = ts[q, k, rr, :]
                fe = jnp.where(
                    wet_e, u_p * c + u_m * eastward(c, rim_e, LANES - 1 - q * K - k), 0.0
                )
                fn = jnp.where(wet_n, v_p * c + v_m * ts[q, k, r + 1 : r + CH + 1, :], 0.0)
                h = pltpu.roll(rim_w, LANES - q * K - k if q else lax.rem(LANES - k, LANES), 1)
                rolled = pltpu.roll(fe, 1, 1)
                fw = jnp.concatenate(
                    [jnp.where(lane == 0, h, rolled[:, :LANES]), rolled[:, LANES:]], axis=1
                )
                fs = jnp.where(row_c == 0, south_row[q], pltpu.roll(fn, 1, 0))
                south_row[q] = fn[CH - 1 : CH, :]
                ns[q, k, rr, :] = jnp.where(wet, c + 0.2 * (fw - fe + fs - fn), 0.0)
        return carry

    first, second = (4 * K) // 10, (8 * K) // 10
    lax.fori_loop(0, first, tracer_level, 0)

    wid_s.wait_recv()
    frc_s.wait_recv()

    @pl.when(not_low)
    def _():
        wid_n.wait_recv()
        frc_n.wait_recv()

    wide_rows = range(0, R + 2 * RIM, CH)
    for r in wide_rows:
        a = jnp.zeros((CH, LANES), F32)
        b = jnp.zeros((CH, LANES), F32)
        for f in range(6):
            mine = (lane >= f * RIM) & (lane < (f + 1) * RIM)
            x0 = w[f, r : r + CH, 0:LANES]
            x1 = w[f, r : r + CH, last:C]
            a = jnp.where(mine, pltpu.roll(x0, f * RIM, 1) if f else x0, a)
            b = jnp.where(mine, pltpu.roll(x1, (RIM + f * RIM) % LANES, 1), b)
        c2w[r : r + CH, :] = a
        c2e[r : r + CH, :] = b
    far_w.start()
    far_e.start()
    lax.fori_loop(first, second, tracer_level, 0)
    far_w.wait_recv()
    far_e.wait_recv()
    for r in wide_rows:
        a, b = r2e[r : r + CH, :], r2w[r : r + CH, :]
        for f in range(6):
            x = pltpu.roll(a, LANES - f * RIM, 1) if f else a
            y = pltpu.roll(b, (LANES - RIM - f * RIM) % LANES, 1)
            w[f, r : r + CH, C:W] = jnp.where(
                lane < RIM, x, jnp.where(lane >= LANES - RIM, y, 0.0)
            )

    @pl.when(not_top)
    def _():
        row_n.wait_send()
        wid_n.wait_send()
        frc_n.wait_send()

    @pl.when(not_low)
    def _():
        row_s.wait_send()
        wid_s.wait_send()
        frc_s.wait_send()

    lane_w = iota((CH, W), 1)
    row_w = iota((CH, W), 0)

    @pl.when(is_top)
    def _():
        row_f.wait_send()
        wid_f.wait_send()
        frc_f.wait_send()
        fold = slice(c1, c1 + RIM)
        for f in (1, 4):
            w[f, fold, :] = -pltpu.roll(w[f, fold, :], W - 1, 1)
        for f, where in ((2, dd), (5, gg)):
            x = w[f, fold, :]
            where[...] = jnp.where(row_w == 0, w[f, c1 - 1 : c1, :] + x, 0.0)
            w[f, fold, :] = -pltpu.roll(x, RIM - 1, 0)

    def wide_depth(shallow):
        return (shallow * (shallow + 1.0)) * (0.8 / (K * (K + 1)))

    def shifted_rows(ref, f, r, by):
        low = r + by
        if low < 0 or low + CH > R + 2 * RIM:
            return pltpu.roll(ref[f, r : r + CH, :], (-by) % CH, 0)
        return ref[f, low : low + CH, :]

    def surface_step(first_step):
        for r in wide_rows:
            rr = slice(r, r + CH)
            u, v = w[1, rr, :], w[2, rr, :]
            div = u - pltpu.roll(u, 1, 1) + (v - shifted_rows(w, 2, r, -1))
            if r == c1:
                div = div + dd[...]
            new = w[0, rr, :] - 0.5 * div
            if first_step:
                new = jnp.where(w[3, rr, :] > 0.0, new, 0.0)
            w[0, rr, :] = new

    def transport_step(first_step):
        for r in wide_rows:
            rr = slice(r, r + CH)
            s, u, v = w[0, rr, :], w[1, rr, :], w[2, rr, :]
            if first_step:
                level = w[3, rr, :]
                shallow_e = jnp.minimum(level, pltpu.roll(level, W - 1, 1))
                shallow_n = jnp.minimum(level, shifted_rows(w, 3, r, 1))
                ae[rr, :] = wide_depth(shallow_e)
                an[rr, :] = wide_depth(shallow_n)
                u = jnp.where(shallow_e > 0.0, u, 0.0)
                v = jnp.where(shallow_n > 0.0, v, 0.0)
            w[1, rr, :] = u - ae[rr, :] * (pltpu.roll(s, W - 1, 1) - s) - w[4, rr, :]
            w[2, rr, :] = v - an[rr, :] * (shifted_rows(w, 0, r, 1) - s) - w[5, rr, :]

    surface_step(True)
    transport_step(True)
    dd[...] = jnp.where(an[c1 - 1 : c1, :] > 0.0, dd[...], 0.0) - gg[...]

    def substep(i, carry):
        surface_step(False)
        transport_step(False)
        dd[...] = dd[...] - gg[...]
        return carry

    lax.fori_loop(1, NSUB, substep, 0)

    low_tri = (iota((R, R), 0) >= iota((R, R), 1)).astype(F32)
    zonal = w[1, c0:c1, 0:C]
    op_ref[...] = exact_dot(low_tri, zonal)
    tot[...] = jnp.broadcast_to(op_ref[R - 1 : R, :], tot.shape)
    sends = []
    for d in range(1, nlat):
        sends.append(
            remote(
                tot, totr.at[d - 1], tssem.at[d - 1], trsem.at[d - 1],
                {"lat": lax.rem(lat + d, nlat)},
            )
        )
    for send in sends:
        send.start()
    lax.fori_loop(second, K, tracer_level, 0)
    os_ref[...] = w[0, c0:c1, 0:C]
    ou_ref[...] = zonal
    ov_ref[...] = w[2, c0:c1, 0:C]
    south = jnp.zeros((8, C), F32)
    for d in range(1, nlat):
        sends[d - 1].wait_recv()
        south = south + totr[d - 1] * (lat >= d).astype(F32)
    scale = -1.0 / math.sqrt(R * nlat)
    op_ref[...] = (op_ref[...] + south[0:1, :]) * scale
    for send in sends:
        send.wait_send()
    for copy in (col_w, col_e, far_w, far_e):
        copy.wait_send()


def hand_over(*refs):
    half = len(refs) // 2
    copies = [
        pltpu.make_async_copy(refs[i], refs[half + i], refs[-1].at[i]) for i in range(half)
    ]
    for copy in copies:
        copy.start()
    for copy in copies:
        copy.wait()


def body(ocean_state, surface_height, zonal_transport, meridional_transport, land_mask, levels):
    nlat, nlon = lax.axis_size("lat"), lax.axis_size("lon")
    _, K, R, C = ocean_state.shape
    wide = (R + 2 * RIM, C + LANES)
    plane = jax.ShapeDtypeStruct((R, C), F32)
    pack = -(-(3 * K + 1) // 8) * 8
    vm = lambda *shape: pltpu.VMEM(shape, F32)
    dma = lambda n: pltpu.SemaphoreType.DMA((n,))
    args = (ocean_state, surface_height, zonal_transport, meridional_transport, land_mask, levels)
    args = [pltpu.with_memory_space_constraint(x, pltpu.HBM) for x in args]
    results = pl.pallas_call(
        functools.partial(kernel, nlat, nlon, K, R, C),
        out_shape=(jax.ShapeDtypeStruct(ocean_state.shape, F32), plane, plane, plane, plane),
        in_specs=[pl.BlockSpec(memory_space=pltpu.HBM)] * 6,
        out_specs=(pl.BlockSpec(memory_space=pltpu.VMEM),) * 5,
        scratch_shapes=[
            vm(2, K, R + 8, C), vm(2, K, R, C), vm(K, R + 8, C),
            pltpu.VMEM((2, R, C), jnp.int32),
            vm(6, *wide), vm(R, C), vm(R, C), vm(R, LANES), vm(2, K, 1, C),
            vm(R, LANES), vm(R, LANES), vm(R, LANES), vm(R, LANES),
            vm(pack, C), vm(pack, C), vm(pack, C), vm(pack, C), vm(pack, C),
            vm(4, RIM, C), vm(2, RIM, C),
            vm(wide[0], LANES), vm(wide[0], LANES), vm(wide[0], LANES), vm(wide[0], LANES),
            vm(*wide), vm(*wide), vm(RIM, wide[1]), vm(RIM, wide[1]),
            vm(8, C), vm(nlat - 1, 8, C),
            dma(7), dma(10), dma(10), dma(nlat - 1), dma(nlat - 1),
        ],
        compiler_params=pltpu.CompilerParams(
            collective_id=0, has_side_effects=True, vmem_limit_bytes=40 * 1024 * 1024
        ),
        cost_estimate=pl.CostEstimate(
            flops=40_000_000, bytes_accessed=2 * ocean_state.size * 4, transcendentals=0
        ),
    )(*args)
    return pl.pallas_call(
        hand_over,
        out_shape=tuple(pltpu.HBM(x.shape, x.dtype) for x in results),
        in_specs=[pl.BlockSpec(memory_space=pltpu.VMEM)] * 5,
        out_specs=(pl.BlockSpec(memory_space=pltpu.HBM),) * 5,
        scratch_shapes=[dma(5)],
    )(*results)


def solution(mesh):
    cells = P("lat", "lon")
    full = P(None, None, "lat", "lon")
    return jax.shard_map(
        body,
        mesh=mesh,
        in_specs=(full, cells, cells, cells, cells, cells),
        out_specs=(full, cells, cells, cells, cells),
        check_vma=False,
    )
```

```python
import functools
import math

import jax
import jax.numpy as jnp
from jax import lax
from jax.experimental import pallas as pl
from jax.experimental.pallas import tpu as pltpu
from jax.sharding import PartitionSpec as P

NSUB = 10
RIM = 16
CH = 16
LANES = 128
F32 = jnp.float32
MESH = pl.DeviceIdType.MESH


def iota(shape, dim):
    return lax.broadcasted_iota(jnp.int32, shape, dim)


def exact_dot(a, b):
    return jnp.dot(a, b, precision=lax.Precision.HIGHEST, preferred_element_type=F32)


def anti(size):
    return (iota((size, size), 0) + iota((size, size), 1) == size - 1).astype(F32)


def anti_blocks(size, block):
    a, b = iota((size, size), 0), iota((size, size), 1)
    same = (a // block) == (b // block)
    return (same & (a % block + b % block == block - 1)).astype(F32)


def remote(src, dst, send, recv, where):
    return pltpu.make_async_remote_copy(
        src_ref=src, dst_ref=dst, send_sem=send, recv_sem=recv, device_id=where, device_id_type=MESH
    )


def kernel(
    nlat, nlon, K, R, C,
    st_hbm, s_hbm, u_hbm, v_hbm, mask_hbm, lev_hbm,
    ns, os_ref, ou_ref, ov_ref, op_ref,
    ts, uv, pr, ml, w, le, ln, fw0, fs0,
    pcw, pce, re, rw, pkn, pks, rn, rs, fold1, fold4, foldf,
    c2w, c2e, r2e, r2w, ae, an, dd, gg, tot, totr,
    lsem, ssem, rsem, tssem, trsem,
):
    lat, lon = lax.axis_index("lat"), lax.axis_index("lon")
    east, west = lax.rem(lon + 1, nlon), lax.rem(lon + nlon - 1, nlon)
    up, down = lax.rem(lat + 1, nlat), lax.rem(lat + nlat - 1, nlat)
    is_top, is_low = lat == nlat - 1, lat == 0
    not_top, not_low = lat < nlat - 1, lat > 0
    turned = nlon - 1 - lon
    W = C + LANES
    c0, c1 = RIM, RIM + R
    last = C - LANES

    barrier = pltpu.get_barrier_semaphore()
    for d in range(1, nlon):
        pl.semaphore_signal(
            barrier, inc=1, device_id={"lon": lax.rem(lon + d, nlon)}, device_id_type=MESH
        )
    for d in range(1, nlat):
        pl.semaphore_signal(
            barrier, inc=1, device_id={"lat": lax.rem(lat + d, nlat)}, device_id_type=MESH
        )

    loads = [
        pltpu.make_async_copy(mask_hbm, ml.at[0], lsem.at[0]),
        pltpu.make_async_copy(lev_hbm, ml.at[1], lsem.at[1]),
        pltpu.make_async_copy(st_hbm.at[0:2], ts.at[:, :, 0:R, :], lsem.at[2]),
        pltpu.make_async_copy(st_hbm.at[2:4], uv, lsem.at[3]),
        pltpu.make_async_copy(s_hbm, w.at[0, c0:c1, 0:C], lsem.at[4]),
        pltpu.make_async_copy(u_hbm, w.at[1, c0:c1, 0:C], lsem.at[5]),
        pltpu.make_async_copy(v_hbm, w.at[2, c0:c1, 0:C], lsem.at[6]),
    ]
    for load in loads:
        load.start()

    col_w = remote(pcw, re, ssem.at[0], rsem.at[0], {"lon": west})
    col_e = remote(pce, rw, ssem.at[1], rsem.at[1], {"lon": east})
    row_n = remote(pkn, rs, ssem.at[2], rsem.at[2], {"lat": up})
    row_s = remote(pks, rn, ssem.at[3], rsem.at[3], {"lat": down})
    row_f = remote(fold1, rn, ssem.at[2], rsem.at[3], {"lon": turned})
    hi, lo = pl.ds(c1 - RIM, RIM), pl.ds(c0, RIM)
    above, below = pl.ds(c1, RIM), pl.ds(0, RIM)
    cols = pl.ds(0, C)
    four, two = pl.ds(0, 4), pl.ds(4, 2)
    wid_n = remote(w.at[four, hi, cols], w.at[four, below, cols], ssem.at[4], rsem.at[4], {"lat": up})
    wid_s = remote(w.at[four, lo, cols], w.at[four, above, cols], ssem.at[5], rsem.at[5], {"lat": down})
    wid_f = remote(fold4, w.at[four, above, cols], ssem.at[4], rsem.at[5], {"lon": turned})
    frc_n = remote(w.at[two, hi, cols], w.at[two, below, cols], ssem.at[6], rsem.at[6], {"lat": up})
    frc_s = remote(w.at[two, lo, cols], w.at[two, above, cols], ssem.at[7], rsem.at[7], {"lat": down})
    frc_f = remote(foldf, w.at[two, above, cols], ssem.at[6], rsem.at[7], {"lon": turned})
    far_w = remote(c2w, r2e, ssem.at[8], rsem.at[8], {"lon": west})
    far_e = remote(c2e, r2w, ssem.at[9], rsem.at[9], {"lon": east})

    @pl.when(is_low)
    def _():
        w[:, 0:RIM, 0:C] = jnp.zeros((6, RIM, C), F32)
        rs[...] = jnp.zeros(rs.shape, F32)

    dd[...] = jnp.zeros(dd.shape, F32)
    gg[...] = jnp.zeros(gg.shape, F32)

    lane = iota((CH, LANES), 1)
    lane_c = iota((CH, C), 1)
    row_c = iota((CH, C), 0)
    chunks = range(0, R, CH)
    loads[0].wait()
    loads[1].wait()
    for r in chunks:
        level = (ml[0, r : r + CH, :] * ml[1, r : r + CH, :]).astype(F32)
        w[3, c0 + r : c0 + r + CH, 0:C] = level
        l0, l1 = level[:, :LANES], level[:, last:]
        pcw[r : r + CH, :] = jnp.where(lane == 3 * K, pltpu.roll(l0, 3 * K, 1), 0.0)
        pce[r : r + CH, :] = jnp.where(lane == 3 * K, pltpu.roll(l1, 3 * K + 1, 1), 0.0)
    loads[2].wait()
    loads[3].wait()
    per = 2.0 / (K * (K + 1))

    def pressure_level(k, sums):
        kf = k.astype(F32)
        thick = (kf + 1.0) * per
        out = []
        for i, r in enumerate(chunks):
            rr = slice(r, r + CH)
            t, s = ts[0, k, rr, :], ts[1, k, rr, :]
            level = w[3, c0 + r : c0 + r + CH, 0:C]
            weight = jnp.where(kf < level, 0.8 * s - 0.3 * t - 0.04 * t * t, 0.0) * thick
            press = sums[i] + 0.5 * weight
            out.append(sums[i] + weight)
            pr[k, rr, :] = press
            u1 = uv[0, k, rr, last:]
            t0, s0, p0 = t[:, :LANES], s[:, :LANES], press[:, :LANES]
            t1, s1 = t[:, last:], s[:, last:]
            a = pcw[rr, :]
            a = jnp.where(lane == k, pltpu.roll(t0, k, 1), a)
            a = jnp.where(lane == K + k, pltpu.roll(s0, K + k, 1), a)
            a = jnp.where(lane == 2 * K + k, pltpu.roll(p0, 2 * K + k, 1), a)
            pcw[rr, :] = a
            b = pce[rr, :]
            b = jnp.where(lane == k, pltpu.roll(t1, k + 1, 1), b)
            b = jnp.where(lane == K + k, pltpu.roll(s1, K + k + 1, 1), b)
            b = jnp.where(lane == 2 * K + k, pltpu.roll(u1, 2 * K + k + 1, 1), b)
            pce[rr, :] = b
        return tuple(out)

    lax.fori_loop(0, K, pressure_level, tuple(jnp.zeros((CH, C), F32) for _ in chunks))
    for k in range(K):
        pkn[k : k + 1, :] = ts[0, k, R - 1 : R, :]
        pkn[K + k : K + k + 1, :] = ts[1, k, R - 1 : R, :]
        pkn[2 * K + k : 2 * K + k + 1, :] = uv[1, k, R - 1 : R, :]
        pks[k : k + 1, :] = ts[0, k, 0:1, :]
        pks[K + k : K + k + 1, :] = ts[1, k, 0:1, :]
        pks[2 * K + k : 2 * K + k + 1, :] = pr[k, 0:1, :]
    pkn[3 * K : 3 * K + 1, :] = w[3, c1 - 1 : c1, 0:C]
    pks[3 * K : 3 * K + 1, :] = w[3, c0 : c0 + 1, 0:C]

    pl.semaphore_wait(barrier, nlat + nlon - 2)

    @pl.when(is_top)
    def _():
        for k in range(K):
            fold1[k : k + 1, :] = ts[0, k, R - 1 : R, :]
            fold1[K + k : K + k + 1, :] = ts[1, k, R - 1 : R, :]
            fold1[2 * K + k : 2 * K + k + 1, :] = pr[k, R - 1 : R, :]
        fold1[3 * K : 3 * K + 1, :] = w[3, c1 - 1 : c1, 0:C]
        fold1[3 * K + 1 :, :] = jnp.zeros((fold1.shape[0] - 3 * K - 1, C), F32)
        fold1[...] = exact_dot(fold1[...], anti(C))
        row_f.start()

    col_w.start()
    col_e.start()

    @pl.when(not_top)
    def _():
        row_n.start()

    @pl.when(not_low)
    def _():
        row_s.start()

    for load in loads[4:]:
        load.wait()

    @pl.when(not_top)
    def _():
        wid_n.start()

    @pl.when(is_top)
    def _():
        rows4 = jnp.concatenate([w[f, c1 - RIM : c1, 0:C] for f in range(4)], axis=0)
        flipped = exact_dot(exact_dot(anti_blocks(4 * RIM, RIM), rows4), anti(C))
        for f in range(4):
            fold4[f] = flipped[f * RIM : (f + 1) * RIM]
        wid_f.start()

    @pl.when(not_low)
    def _():
        wid_s.start()

    col_w.wait_recv()
    row_s.wait_recv()
    for k in range(K):
        ts[0, k, R : R + 1, :] = rn[k : k + 1, :]
        ts[1, k, R : R + 1, :] = rn[K + k : K + k + 1, :]
        pr[k, R : R + 1, :] = rn[2 * K + k : 2 * K + k + 1, :]

    def eastward(centre, rim, shift):
        rolled = pltpu.roll(centre, C - 1, 1)
        h = pltpu.roll(rim, shift, 1)
        edge = jnp.where(lane == LANES - 1, h, rolled[:, last:])
        return jnp.concatenate([rolled[:, :last], edge], axis=1)

    for r in chunks:
        level = w[3, c0 + r : c0 + r + CH, 0:C]
        le[r : r + CH, :] = jnp.minimum(
            level, eastward(level, re[r : r + CH, :], LANES - 1 - 3 * K)
        )
        if r + CH < R:
            north = w[3, c0 + r + 1 : c0 + r + CH + 1, 0:C]
        else:
            north = jnp.where(
                row_c == CH - 1, rn[3 * K : 3 * K + 1, :], pltpu.roll(level, CH - 1, 0)
            )
        ln[r : r + CH, :] = jnp.minimum(level, north)

    for r in chunks:
        rr = slice(r, r + CH)
        le_r, ln_r, rim = le[rr, :], ln[rr, :], re[rr, :]

        def force_level(k, sums):
            fx, fy = sums
            kf = k.astype(F32)
            thick = (kf + 1.0) * per
            press = pr[k, rr, :]
            p_e = eastward(press, rim, LANES - 1 - 2 * K - k)
            p_n = pr[k, r + 1 : r + CH + 1, :]
            open_e, open_n = kf < le_r, kf < ln_r
            gx = jnp.where(open_e, p_e - press, 0.0)
            gy = jnp.where(open_n, p_n - press, 0.0)
            ns[2, k, rr, :] = jnp.where(open_e, uv[0, k, rr, :] - 0.2 * gx, 0.0)
            ns[3, k, rr, :] = jnp.where(open_n, uv[1, k, rr, :] - 0.2 * gy, 0.0)
            return fx + gx * thick, fy + gy * thick

        zero = jnp.zeros((CH, C), F32)
        fx, fy = lax.fori_loop(0, K, force_level, (zero, zero))
        w[4, c0 + r : c0 + r + CH, 0:C] = 0.1 * fx
        w[5, c0 + r : c0 + r + CH, 0:C] = 0.1 * fy

    @pl.when(not_top)
    def _():
        frc_n.start()

    @pl.when(is_top)
    def _():
        rows2 = jnp.concatenate([w[f, c1 - RIM : c1, 0:C] for f in (4, 5)], axis=0)
        flipped = exact_dot(exact_dot(anti_blocks(2 * RIM, RIM), rows2), anti(C))
        foldf[0] = flipped[:RIM]
        foldf[1] = flipped[RIM:]
        frc_f.start()

    @pl.when(not_low)
    def _():
        frc_s.start()

    col_e.wait_recv()

    @pl.when(not_low)
    def _():
        row_n.wait_recv()

    lane_f = jnp.where(lane < K, lane, lane - K).astype(F32)
    for r in chunks:
        rr = slice(r, r + CH)
        a, b = rw[rr, :], pcw[rr, :]
        u = jnp.where(lane < K, pltpu.roll(a, LANES - 2 * K, 1), pltpu.roll(a, LANES - K, 1))
        shallow = jnp.minimum(a[:, 3 * K : 3 * K + 1], b[:, 3 * K : 3 * K + 1])
        flux = (jnp.maximum(u, 0.0) + 0.1) * a + (jnp.minimum(u, 0.0) - 0.1) * b
        fw0[rr, :] = jnp.where(lane_f < shallow, flux, 0.0)
    row_k = iota((K, C), 0).astype(F32)
    shallow = jnp.minimum(rs[3 * K : 3 * K + 1, :], pks[3 * K : 3 * K + 1, :])
    v_rim = rs[2 * K : 3 * K, :]
    vp, vm = jnp.maximum(v_rim, 0.0) + 0.1, jnp.minimum(v_rim, 0.0) - 0.1
    for q in range(2):
        flux = vp * rs[q * K : (q + 1) * K, :] + vm * pks[q * K : (q + 1) * K, :]
        flux = jnp.where(row_k < shallow, flux, 0.0)
        for k in range(K):
            fs0[q, k] = flux[k : k + 1, :]

    def tracer_level(k, carry):
        kf = k.astype(F32)
        south_row = [fs0[q, k] for q in range(2)]
        for r in chunks:
            rr = slice(r, r + CH)
            u, v = uv[0, k, rr, :], uv[1, k, rr, :]
            u_p, u_m = jnp.maximum(u, 0.0) + 0.1, jnp.minimum(u, 0.0) - 0.1
            v_p, v_m = jnp.maximum(v, 0.0) + 0.1, jnp.minimum(v, 0.0) - 0.1
            wet = kf < w[3, c0 + r : c0 + r + CH, 0:C]
            wet_e, wet_n = kf < le[rr, :], kf < ln[rr, :]
            rim_e, rim_w = re[rr, :], fw0[rr, :]
            for q in range(2):
                c = ts[q, k, rr, :]
                fe = jnp.where(
                    wet_e, u_p * c + u_m * eastward(c, rim_e, LANES - 1 - q * K - k), 0.0
                )
                fn = jnp.where(wet_n, v_p * c + v_m * ts[q, k, r + 1 : r + CH + 1, :], 0.0)
                h = pltpu.roll(rim_w, LANES - q * K - k if q else lax.rem(LANES - k, LANES), 1)
                rolled = pltpu.roll(fe, 1, 1)
                fw = jnp.concatenate(
                    [jnp.where(lane == 0, h, rolled[:, :LANES]), rolled[:, LANES:]], axis=1
                )
                fs = jnp.where(row_c == 0, south_row[q], pltpu.roll(fn, 1, 0))
                south_row[q] = fn[CH - 1 : CH, :]
                ns[q, k, rr, :] = jnp.where(wet, c + 0.2 * (fw - fe + fs - fn), 0.0)
        return carry

    first, second = (4 * K) // 10, (8 * K) // 10
    lax.fori_loop(0, first, tracer_level, 0)

    wid_s.wait_recv()
    frc_s.wait_recv()

    @pl.when(not_low)
    def _():
        wid_n.wait_recv()
        frc_n.wait_recv()

    wide_rows = range(0, R + 2 * RIM, CH)
    for r in wide_rows:
        a = jnp.zeros((CH, LANES), F32)
        b = jnp.zeros((CH, LANES), F32)
        for f in range(6):
            mine = (lane >= f * RIM) & (lane < (f + 1) * RIM)
            x0 = w[f, r : r + CH, 0:LANES]
            x1 = w[f, r : r + CH, last:C]
            a = jnp.where(mine, pltpu.roll(x0, f * RIM, 1) if f else x0, a)
            b = jnp.where(mine, pltpu.roll(x1, (RIM + f * RIM) % LANES, 1), b)
        c2w[r : r + CH, :] = a
        c2e[r : r + CH, :] = b
    far_w.start()
    far_e.start()
    lax.fori_loop(first, second, tracer_level, 0)
    far_w.wait_recv()
    far_e.wait_recv()
    for r in wide_rows:
        a, b = r2e[r : r + CH, :], r2w[r : r + CH, :]
        for f in range(6):
            x = pltpu.roll(a, LANES - f * RIM, 1) if f else a
            y = pltpu.roll(b, (LANES - RIM - f * RIM) % LANES, 1)
            w[f, r : r + CH, C:W] = jnp.where(
                lane < RIM, x, jnp.where(lane >= LANES - RIM, y, 0.0)
            )

    @pl.when(not_top)
    def _():
        row_n.wait_send()
        wid_n.wait_send()
        frc_n.wait_send()

    @pl.when(not_low)
    def _():
        row_s.wait_send()
        wid_s.wait_send()
        frc_s.wait_send()

    lane_w = iota((CH, W), 1)
    row_w = iota((CH, W), 0)

    @pl.when(is_top)
    def _():
        row_f.wait_send()
        wid_f.wait_send()
        frc_f.wait_send()
        fold = slice(c1, c1 + RIM)
        for f in (1, 4):
            w[f, fold, :] = -pltpu.roll(w[f, fold, :], W - 1, 1)
        for f, where in ((2, dd), (5, gg)):
            x = w[f, fold, :]
            where[...] = jnp.where(row_w == 0, w[f, c1 - 1 : c1, :] + x, 0.0)
            w[f, fold, :] = -pltpu.roll(x, RIM - 1, 0)

    def wide_depth(shallow):
        return (shallow * (shallow + 1.0)) * (0.8 / (K * (K + 1)))

    def shifted_rows(ref, f, r, by):
        low = r + by
        if low < 0 or low + CH > R + 2 * RIM:
            return pltpu.roll(ref[f, r : r + CH, :], (-by) % CH, 0)
        return ref[f, low : low + CH, :]

    def surface_step(first_step):
        for r in wide_rows:
            rr = slice(r, r + CH)
            u, v = w[1, rr, :], w[2, rr, :]
            div = u - pltpu.roll(u, 1, 1) + (v - shifted_rows(w, 2, r, -1))
            if r == c1:
                div = div + dd[...]
            new = w[0, rr, :] - 0.5 * div
            if first_step:
                new = jnp.where(w[3, rr, :] > 0.0, new, 0.0)
            w[0, rr, :] = new

    def transport_step(first_step):
        for r in wide_rows:
            rr = slice(r, r + CH)
            s, u, v = w[0, rr, :], w[1, rr, :], w[2, rr, :]
            if first_step:
                level = w[3, rr, :]
                shallow_e = jnp.minimum(level, pltpu.roll(level, W - 1, 1))
                shallow_n = jnp.minimum(level, shifted_rows(w, 3, r, 1))
                ae[rr, :] = wide_depth(shallow_e)
                an[rr, :] = wide_depth(shallow_n)
                u = jnp.where(shallow_e > 0.0, u, 0.0)
                v = jnp.where(shallow_n > 0.0, v, 0.0)
            w[1, rr, :] = u - ae[rr, :] * (pltpu.roll(s, W - 1, 1) - s) - w[4, rr, :]
            w[2, rr, :] = v - an[rr, :] * (shifted_rows(w, 0, r, 1) - s) - w[5, rr, :]

    surface_step(True)
    transport_step(True)
    dd[...] = jnp.where(an[c1 - 1 : c1, :] > 0.0, dd[...], 0.0) - gg[...]

    def substep(i, carry):
        surface_step(False)
        transport_step(False)
        dd[...] = dd[...] - gg[...]
        return carry

    lax.fori_loop(1, NSUB, substep, 0)

    low_tri = (iota((R, R), 0) >= iota((R, R), 1)).astype(F32)
    zonal = w[1, c0:c1, 0:C]
    op_ref[...] = exact_dot(low_tri, zonal)
    tot[...] = jnp.broadcast_to(op_ref[R - 1 : R, :], tot.shape)
    sends = []
    for d in range(1, nlat):
        sends.append(
            remote(
                tot, totr.at[d - 1], tssem.at[d - 1], trsem.at[d - 1],
                {"lat": lax.rem(lat + d, nlat)},
            )
        )
    for send in sends:
        send.start()
    lax.fori_loop(second, K, tracer_level, 0)
    os_ref[...] = w[0, c0:c1, 0:C]
    ou_ref[...] = zonal
    ov_ref[...] = w[2, c0:c1, 0:C]
    south = jnp.zeros((8, C), F32)
    for d in range(1, nlat):
        sends[d - 1].wait_recv()
        south = south + totr[d - 1] * (lat >= d).astype(F32)
    scale = -1.0 / math.sqrt(R * nlat)
    op_ref[...] = (op_ref[...] + south[0:1, :]) * scale
    for send in sends:
        send.wait_send()
    for copy in (col_w, col_e, far_w, far_e):
        copy.wait_send()


def hand_over(*refs):
    half = len(refs) // 2
    copies = [
        pltpu.make_async_copy(refs[i], refs[half + i], refs[-1].at[i]) for i in range(half)
    ]
    for copy in copies:
        copy.start()
    for copy in copies:
        copy.wait()


def body(ocean_state, surface_height, zonal_transport, meridional_transport, land_mask, levels):
    nlat, nlon = lax.axis_size("lat"), lax.axis_size("lon")
    _, K, R, C = ocean_state.shape
    wide = (R + 2 * RIM, C + LANES)
    plane = jax.ShapeDtypeStruct((R, C), F32)
    pack = -(-(3 * K + 1) // 8) * 8
    vm = lambda *shape: pltpu.VMEM(shape, F32)
    dma = lambda n: pltpu.SemaphoreType.DMA((n,))
    args = (ocean_state, surface_height, zonal_transport, meridional_transport, land_mask, levels)
    args = [pltpu.with_memory_space_constraint(x, pltpu.HBM) for x in args]
    results = pl.pallas_call(
        functools.partial(kernel, nlat, nlon, K, R, C),
        out_shape=(jax.ShapeDtypeStruct(ocean_state.shape, F32), plane, plane, plane, plane),
        in_specs=[pl.BlockSpec(memory_space=pltpu.HBM)] * 6,
        out_specs=(pl.BlockSpec(memory_space=pltpu.VMEM),) * 5,
        scratch_shapes=[
            vm(2, K, R + 8, C), vm(2, K, R, C), vm(K, R + 8, C),
            pltpu.VMEM((2, R, C), jnp.int32),
            vm(6, *wide), vm(R, C), vm(R, C), vm(R, LANES), vm(2, K, 1, C),
            vm(R, LANES), vm(R, LANES), vm(R, LANES), vm(R, LANES),
            vm(pack, C), vm(pack, C), vm(pack, C), vm(pack, C), vm(pack, C),
            vm(4, RIM, C), vm(2, RIM, C),
            vm(wide[0], LANES), vm(wide[0], LANES), vm(wide[0], LANES), vm(wide[0], LANES),
            vm(*wide), vm(*wide), vm(RIM, wide[1]), vm(RIM, wide[1]),
            vm(8, C), vm(nlat - 1, 8, C),
            dma(7), dma(10), dma(10), dma(nlat - 1), dma(nlat - 1),
        ],
        compiler_params=pltpu.CompilerParams(
            collective_id=0, has_side_effects=True, vmem_limit_bytes=40 * 1024 * 1024
        ),
        cost_estimate=pl.CostEstimate(
            flops=40_000_000, bytes_accessed=2 * ocean_state.size * 4, transcendentals=0
        ),
    )(*args)
    return pl.pallas_call(
        hand_over,
        out_shape=tuple(pltpu.HBM(x.shape, x.dtype) for x in results),
        in_specs=[pl.BlockSpec(memory_space=pltpu.VMEM)] * 5,
        out_specs=(pl.BlockSpec(memory_space=pltpu.HBM),) * 5,
        scratch_shapes=[dma(5)],
        compiler_params=pltpu.CompilerParams(vmem_limit_bytes=4 * 1024 * 1024),
    )(*[pltpu.with_memory_space_constraint(x, pltpu.VMEM) for x in results])


def solution(mesh):
    cells = P("lat", "lon")
    full = P(None, None, "lat", "lon")
    return jax.shard_map(
        body,
        mesh=mesh,
        in_specs=(full, cells, cells, cells, cells, cells),
        out_specs=(full, cells, cells, cells, cells),
        check_vma=False,
    )
```

```python
import functools
import math

import jax
import jax.numpy as jnp
from jax import lax
from jax.experimental import pallas as pl
from jax.experimental.pallas import tpu as pltpu
from jax.sharding import PartitionSpec as P

NSUB = 10
RIM = 16
CH = 16
LANES = 128
F32 = jnp.float32
MESH = pl.DeviceIdType.MESH


def iota(shape, dim):
    return lax.broadcasted_iota(jnp.int32, shape, dim)


def exact_dot(a, b):
    return jnp.dot(a, b, precision=lax.Precision.HIGHEST, preferred_element_type=F32)


def anti(size):
    return (iota((size, size), 0) + iota((size, size), 1) == size - 1).astype(F32)


def anti_blocks(size, block):
    a, b = iota((size, size), 0), iota((size, size), 1)
    same = (a // block) == (b // block)
    return (same & (a % block + b % block == block - 1)).astype(F32)


def remote(src, dst, send, recv, where):
    return pltpu.make_async_remote_copy(
        src_ref=src, dst_ref=dst, send_sem=send, recv_sem=recv, device_id=where, device_id_type=MESH
    )


def kernel(
    nlat, nlon, K, R, C,
    st_hbm, s_hbm, u_hbm, v_hbm, mask_hbm, lev_hbm,
    ns, os_ref, ou_ref, ov_ref, op_ref,
    ts, uv, pr, ml, w, le, ln, fw0, fs0,
    pcw, pce, re, rw, pkn, pks, rn, rs, fold1, fold4, foldf,
    c2w, c2e, r2e, r2w, ae, an, dd, gg, tot, tot2, totr,
    lsem, ssem, rsem, tssem, trsem,
):
    lat, lon = lax.axis_index("lat"), lax.axis_index("lon")
    east, west = lax.rem(lon + 1, nlon), lax.rem(lon + nlon - 1, nlon)
    up, down = lax.rem(lat + 1, nlat), lax.rem(lat + nlat - 1, nlat)
    is_top, is_low = lat == nlat - 1, lat == 0
    not_top, not_low = lat < nlat - 1, lat > 0
    turned = nlon - 1 - lon
    W = C + LANES
    c0, c1 = RIM, RIM + R
    last = C - LANES

    barrier = pltpu.get_barrier_semaphore()
    for d in range(1, nlon):
        pl.semaphore_signal(
            barrier, inc=1, device_id={"lon": lax.rem(lon + d, nlon)}, device_id_type=MESH
        )
    for d in range(1, nlat):
        pl.semaphore_signal(
            barrier, inc=1, device_id={"lat": lax.rem(lat + d, nlat)}, device_id_type=MESH
        )

    loads = [
        pltpu.make_async_copy(mask_hbm, ml.at[0], lsem.at[0]),
        pltpu.make_async_copy(lev_hbm, ml.at[1], lsem.at[1]),
        pltpu.make_async_copy(st_hbm.at[0:2], ts.at[:, :, 0:R, :], lsem.at[2]),
        pltpu.make_async_copy(st_hbm.at[2:4], uv, lsem.at[3]),
        pltpu.make_async_copy(s_hbm, w.at[0, c0:c1, 0:C], lsem.at[4]),
        pltpu.make_async_copy(u_hbm, w.at[1, c0:c1, 0:C], lsem.at[5]),
        pltpu.make_async_copy(v_hbm, w.at[2, c0:c1, 0:C], lsem.at[6]),
    ]
    for load in loads:
        load.start()

    col_w = remote(pcw, re, ssem.at[0], rsem.at[0], {"lon": west})
    col_e = remote(pce, rw, ssem.at[1], rsem.at[1], {"lon": east})
    row_n = remote(pkn, rs, ssem.at[2], rsem.at[2], {"lat": up})
    row_s = remote(pks, rn, ssem.at[3], rsem.at[3], {"lat": down})
    row_f = remote(fold1, rn, ssem.at[2], rsem.at[3], {"lon": turned})
    hi, lo = pl.ds(c1 - RIM, RIM), pl.ds(c0, RIM)
    above, below = pl.ds(c1, RIM), pl.ds(0, RIM)
    cols = pl.ds(0, C)
    four, two = pl.ds(0, 4), pl.ds(4, 2)
    wid_n = remote(w.at[four, hi, cols], w.at[four, below, cols], ssem.at[4], rsem.at[4], {"lat": up})
    wid_s = remote(w.at[four, lo, cols], w.at[four, above, cols], ssem.at[5], rsem.at[5], {"lat": down})
    wid_f = remote(fold4, w.at[four, above, cols], ssem.at[4], rsem.at[5], {"lon": turned})
    frc_n = remote(w.at[two, hi, cols], w.at[two, below, cols], ssem.at[6], rsem.at[6], {"lat": up})
    frc_s = remote(w.at[two, lo, cols], w.at[two, above, cols], ssem.at[7], rsem.at[7], {"lat": down})
    frc_f = remote(foldf, w.at[two, above, cols], ssem.at[6], rsem.at[7], {"lon": turned})
    far_w = remote(c2w, r2e, ssem.at[8], rsem.at[8], {"lon": west})
    far_e = remote(c2e, r2w, ssem.at[9], rsem.at[9], {"lon": east})

    @pl.when(is_low)
    def _():
        w[:, 0:RIM, 0:C] = jnp.zeros((6, RIM, C), F32)
        rs[...] = jnp.zeros(rs.shape, F32)

    dd[...] = jnp.zeros(dd.shape, F32)
    gg[...] = jnp.zeros(gg.shape, F32)

    lane = iota((CH, LANES), 1)
    lane_c = iota((CH, C), 1)
    row_c = iota((CH, C), 0)
    chunks = range(0, R, CH)
    loads[0].wait()
    loads[1].wait()
    for r in chunks:
        level = (ml[0, r : r + CH, :] * ml[1, r : r + CH, :]).astype(F32)
        w[3, c0 + r : c0 + r + CH, 0:C] = level
        l0, l1 = level[:, :LANES], level[:, last:]
        pcw[r : r + CH, :] = jnp.where(lane == 3 * K, pltpu.roll(l0, 3 * K, 1), 0.0)
        pce[r : r + CH, :] = jnp.where(lane == 3 * K, pltpu.roll(l1, 3 * K + 1, 1), 0.0)
    loads[2].wait()
    loads[3].wait()
    per = 2.0 / (K * (K + 1))

    def pressure_level(k, sums):
        kf = k.astype(F32)
        thick = (kf + 1.0) * per
        out = []
        for i, r in enumerate(chunks):
            rr = slice(r, r + CH)
            t, s = ts[0, k, rr, :], ts[1, k, rr, :]
            level = w[3, c0 + r : c0 + r + CH, 0:C]
            weight = jnp.where(kf < level, 0.8 * s - 0.3 * t - 0.04 * t * t, 0.0) * thick
            press = sums[i] + 0.5 * weight
            out.append(sums[i] + weight)
            pr[k, rr, :] = press
            u1 = uv[0, k, rr, last:]
            t0, s0, p0 = t[:, :LANES], s[:, :LANES], press[:, :LANES]
            t1, s1 = t[:, last:], s[:, last:]
            a = pcw[rr, :]
            a = jnp.where(lane == k, pltpu.roll(t0, k, 1), a)
            a = jnp.where(lane == K + k, pltpu.roll(s0, K + k, 1), a)
            a = jnp.where(lane == 2 * K + k, pltpu.roll(p0, 2 * K + k, 1), a)
            pcw[rr, :] = a
            b = pce[rr, :]
            b = jnp.where(lane == k, pltpu.roll(t1, k + 1, 1), b)
            b = jnp.where(lane == K + k, pltpu.roll(s1, K + k + 1, 1), b)
            b = jnp.where(lane == 2 * K + k, pltpu.roll(u1, 2 * K + k + 1, 1), b)
            pce[rr, :] = b
        return tuple(out)

    lax.fori_loop(0, K, pressure_level, tuple(jnp.zeros((CH, C), F32) for _ in chunks), unroll=2)
    for k in range(K):
        pkn[k : k + 1, :] = ts[0, k, R - 1 : R, :]
        pkn[K + k : K + k + 1, :] = ts[1, k, R - 1 : R, :]
        pkn[2 * K + k : 2 * K + k + 1, :] = uv[1, k, R - 1 : R, :]
        pks[k : k + 1, :] = ts[0, k, 0:1, :]
        pks[K + k : K + k + 1, :] = ts[1, k, 0:1, :]
        pks[2 * K + k : 2 * K + k + 1, :] = pr[k, 0:1, :]
    pkn[3 * K : 3 * K + 1, :] = w[3, c1 - 1 : c1, 0:C]
    pks[3 * K : 3 * K + 1, :] = w[3, c0 : c0 + 1, 0:C]

    pl.semaphore_wait(barrier, nlat + nlon - 2)

    @pl.when(is_top)
    def _():
        for k in range(K):
            fold1[k : k + 1, :] = ts[0, k, R - 1 : R, :]
            fold1[K + k : K + k + 1, :] = ts[1, k, R - 1 : R, :]
            fold1[2 * K + k : 2 * K + k + 1, :] = pr[k, R - 1 : R, :]
        fold1[3 * K : 3 * K + 1, :] = w[3, c1 - 1 : c1, 0:C]
        fold1[3 * K + 1 :, :] = jnp.zeros((fold1.shape[0] - 3 * K - 1, C), F32)
        fold1[...] = exact_dot(fold1[...], anti(C))
        row_f.start()

    col_w.start()
    col_e.start()

    @pl.when(not_top)
    def _():
        row_n.start()

    @pl.when(not_low)
    def _():
        row_s.start()

    for load in loads[4:]:
        load.wait()

    @pl.when(not_top)
    def _():
        wid_n.start()

    @pl.when(is_top)
    def _():
        rows4 = jnp.concatenate([w[f, c1 - RIM : c1, 0:C] for f in range(4)], axis=0)
        flipped = exact_dot(exact_dot(anti_blocks(4 * RIM, RIM), rows4), anti(C))
        for f in range(4):
            fold4[f] = flipped[f * RIM : (f + 1) * RIM]
        wid_f.start()

    @pl.when(not_low)
    def _():
        wid_s.start()

    col_w.wait_recv()
    row_s.wait_recv()
    for k in range(K):
        ts[0, k, R : R + 1, :] = rn[k : k + 1, :]
        ts[1, k, R : R + 1, :] = rn[K + k : K + k + 1, :]
        pr[k, R : R + 1, :] = rn[2 * K + k : 2 * K + k + 1, :]

    def eastward(centre, rim, shift):
        rolled = pltpu.roll(centre, C - 1, 1)
        h = pltpu.roll(rim, shift, 1)
        edge = jnp.where(lane == LANES - 1, h, rolled[:, last:])
        return jnp.concatenate([rolled[:, :last], edge], axis=1)

    for r in chunks:
        level = w[3, c0 + r : c0 + r + CH, 0:C]
        le[r : r + CH, :] = jnp.minimum(
            level, eastward(level, re[r : r + CH, :], LANES - 1 - 3 * K)
        )
        if r + CH < R:
            north = w[3, c0 + r + 1 : c0 + r + CH + 1, 0:C]
        else:
            north = jnp.where(
                row_c == CH - 1, rn[3 * K : 3 * K + 1, :], pltpu.roll(level, CH - 1, 0)
            )
        ln[r : r + CH, :] = jnp.minimum(level, north)

    for r in chunks:
        rr = slice(r, r + CH)
        le_r, ln_r, rim = le[rr, :], ln[rr, :], re[rr, :]

        def force_level(k, sums):
            fx, fy = sums
            kf = k.astype(F32)
            thick = (kf + 1.0) * per
            press = pr[k, rr, :]
            p_e = eastward(press, rim, LANES - 1 - 2 * K - k)
            p_n = pr[k, r + 1 : r + CH + 1, :]
            open_e, open_n = kf < le_r, kf < ln_r
            gx = jnp.where(open_e, p_e - press, 0.0)
            gy = jnp.where(open_n, p_n - press, 0.0)
            ns[2, k, rr, :] = jnp.where(open_e, uv[0, k, rr, :] - 0.2 * gx, 0.0)
            ns[3, k, rr, :] = jnp.where(open_n, uv[1, k, rr, :] - 0.2 * gy, 0.0)
            return fx + gx * thick, fy + gy * thick

        zero = jnp.zeros((CH, C), F32)
        fx, fy = lax.fori_loop(0, K, force_level, (zero, zero), unroll=5)
        w[4, c0 + r : c0 + r + CH, 0:C] = 0.1 * fx
        w[5, c0 + r : c0 + r + CH, 0:C] = 0.1 * fy

    @pl.when(not_top)
    def _():
        frc_n.start()

    @pl.when(is_top)
    def _():
        rows2 = jnp.concatenate([w[f, c1 - RIM : c1, 0:C] for f in (4, 5)], axis=0)
        flipped = exact_dot(exact_dot(anti_blocks(2 * RIM, RIM), rows2), anti(C))
        foldf[0] = flipped[:RIM]
        foldf[1] = flipped[RIM:]
        frc_f.start()

    @pl.when(not_low)
    def _():
        frc_s.start()

    col_e.wait_recv()

    @pl.when(not_low)
    def _():
        row_n.wait_recv()

    lane_f = jnp.where(lane < K, lane, lane - K).astype(F32)
    for r in chunks:
        rr = slice(r, r + CH)
        a, b = rw[rr, :], pcw[rr, :]
        u = jnp.where(lane < K, pltpu.roll(a, LANES - 2 * K, 1), pltpu.roll(a, LANES - K, 1))
        shallow = jnp.minimum(a[:, 3 * K : 3 * K + 1], b[:, 3 * K : 3 * K + 1])
        flux = (jnp.maximum(u, 0.0) + 0.1) * a + (jnp.minimum(u, 0.0) - 0.1) * b
        fw0[rr, :] = jnp.where(lane_f < shallow, flux, 0.0)
    row_k = iota((K, C), 0).astype(F32)
    shallow = jnp.minimum(rs[3 * K : 3 * K + 1, :], pks[3 * K : 3 * K + 1, :])
    v_rim = rs[2 * K : 3 * K, :]
    vp, vm = jnp.maximum(v_rim, 0.0) + 0.1, jnp.minimum(v_rim, 0.0) - 0.1
    for q in range(2):
        flux = vp * rs[q * K : (q + 1) * K, :] + vm * pks[q * K : (q + 1) * K, :]
        flux = jnp.where(row_k < shallow, flux, 0.0)
        for k in range(K):
            fs0[q, k] = flux[k : k + 1, :]

    def tracer_level(k, carry):
        kf = k.astype(F32)
        south_row = [fs0[q, k] for q in range(2)]
        for r in chunks:
            rr = slice(r, r + CH)
            u, v = uv[0, k, rr, :], uv[1, k, rr, :]
            u_p, u_m = jnp.maximum(u, 0.0) + 0.1, jnp.minimum(u, 0.0) - 0.1
            v_p, v_m = jnp.maximum(v, 0.0) + 0.1, jnp.minimum(v, 0.0) - 0.1
            wet = kf < w[3, c0 + r : c0 + r + CH, 0:C]
            wet_e, wet_n = kf < le[rr, :], kf < ln[rr, :]
            rim_e, rim_w = re[rr, :], fw0[rr, :]
            for q in range(2):
                c = ts[q, k, rr, :]
                fe = jnp.where(
                    wet_e, u_p * c + u_m * eastward(c, rim_e, LANES - 1 - q * K - k), 0.0
                )
                fn = jnp.where(wet_n, v_p * c + v_m * ts[q, k, r + 1 : r + CH + 1, :], 0.0)
                h = pltpu.roll(rim_w, LANES - q * K - k if q else lax.rem(LANES - k, LANES), 1)
                rolled = pltpu.roll(fe, 1, 1)
                fw = jnp.concatenate(
                    [jnp.where(lane == 0, h, rolled[:, :LANES]), rolled[:, LANES:]], axis=1
                )
                fs = jnp.where(row_c == 0, south_row[q], pltpu.roll(fn, 1, 0))
                south_row[q] = fn[CH - 1 : CH, :]
                ns[q, k, rr, :] = jnp.where(wet, c + 0.2 * (fw - fe + fs - fn), 0.0)
        return carry

    first, second = (4 * K) // 10, (8 * K) // 10
    lax.fori_loop(0, first, tracer_level, 0)

    wid_s.wait_recv()
    frc_s.wait_recv()

    @pl.when(not_low)
    def _():
        wid_n.wait_recv()
        frc_n.wait_recv()

    wide_rows = range(0, R + 2 * RIM, CH)
    for r in wide_rows:
        a = jnp.zeros((CH, LANES), F32)
        b = jnp.zeros((CH, LANES), F32)
        for f in range(6):
            mine = (lane >= f * RIM) & (lane < (f + 1) * RIM)
            x0 = w[f, r : r + CH, 0:LANES]
            x1 = w[f, r : r + CH, last:C]
            a = jnp.where(mine, pltpu.roll(x0, f * RIM, 1) if f else x0, a)
            b = jnp.where(mine, pltpu.roll(x1, (RIM + f * RIM) % LANES, 1), b)
        c2w[r : r + CH, :] = a
        c2e[r : r + CH, :] = b
    far_w.start()
    far_e.start()
    lax.fori_loop(first, second, tracer_level, 0)
    far_w.wait_recv()
    far_e.wait_recv()
    for r in wide_rows:
        a, b = r2e[r : r + CH, :], r2w[r : r + CH, :]
        for f in range(6):
            x = pltpu.roll(a, LANES - f * RIM, 1) if f else a
            y = pltpu.roll(b, (LANES - RIM - f * RIM) % LANES, 1)
            w[f, r : r + CH, C:W] = jnp.where(
                lane < RIM, x, jnp.where(lane >= LANES - RIM, y, 0.0)
            )

    @pl.when(not_top)
    def _():
        row_n.wait_send()
        wid_n.wait_send()
        frc_n.wait_send()

    @pl.when(not_low)
    def _():
        row_s.wait_send()
        wid_s.wait_send()
        frc_s.wait_send()

    lane_w = iota((CH, W), 1)
    row_w = iota((CH, W), 0)

    @pl.when(is_top)
    def _():
        row_f.wait_send()
        wid_f.wait_send()
        frc_f.wait_send()
        fold = slice(c1, c1 + RIM)
        for f in (1, 4):
            w[f, fold, :] = -pltpu.roll(w[f, fold, :], W - 1, 1)
        for f, where in ((2, dd), (5, gg)):
            x = w[f, fold, :]
            where[...] = jnp.where(row_w == 0, w[f, c1 - 1 : c1, :] + x, 0.0)
            w[f, fold, :] = -pltpu.roll(x, RIM - 1, 0)

    def wide_depth(shallow):
        return (shallow * (shallow + 1.0)) * (0.8 / (K * (K + 1)))

    def shifted_rows(ref, f, r, by):
        low = r + by
        if low < 0 or low + CH > R + 2 * RIM:
            return pltpu.roll(ref[f, r : r + CH, :], (-by) % CH, 0)
        return ref[f, low : low + CH, :]

    def surface_step(first_step):
        for r in wide_rows:
            rr = slice(r, r + CH)
            u, v = w[1, rr, :], w[2, rr, :]
            div = u - pltpu.roll(u, 1, 1) + (v - shifted_rows(w, 2, r, -1))
            if r == c1:
                div = div + dd[...]
            new = w[0, rr, :] - 0.5 * div
            if first_step:
                new = jnp.where(w[3, rr, :] > 0.0, new, 0.0)
            w[0, rr, :] = new

    def transport_step(first_step):
        for r in wide_rows:
            rr = slice(r, r + CH)
            s, u, v = w[0, rr, :], w[1, rr, :], w[2, rr, :]
            if first_step:
                level = w[3, rr, :]
                shallow_e = jnp.minimum(level, pltpu.roll(level, W - 1, 1))
                shallow_n = jnp.minimum(level, shifted_rows(w, 3, r, 1))
                ae[rr, :] = wide_depth(shallow_e)
                an[rr, :] = wide_depth(shallow_n)
                u = jnp.where(shallow_e > 0.0, u, 0.0)
                v = jnp.where(shallow_n > 0.0, v, 0.0)
            w[1, rr, :] = u - ae[rr, :] * (pltpu.roll(s, W - 1, 1) - s) - w[4, rr, :]
            w[2, rr, :] = v - an[rr, :] * (shifted_rows(w, 0, r, 1) - s) - w[5, rr, :]

    surface_step(True)
    transport_step(True)
    dd[...] = jnp.where(an[c1 - 1 : c1, :] > 0.0, dd[...], 0.0) - gg[...]

    def substep(i, carry):
        surface_step(False)
        transport_step(False)
        dd[...] = dd[...] - gg[...]
        return carry

    lax.fori_loop(1, NSUB, substep, 0)

    low_tri = (iota((R, R), 0) >= iota((R, R), 1)).astype(F32)
    zonal = w[1, c0:c1, 0:C]
    op_ref[...] = exact_dot(low_tri, zonal)
    tot[...] = op_ref[R - 1 : R, :]
    sends = []
    for d in range(1, nlat):
        sends.append(
            remote(
                tot, totr.at[d - 1], tssem.at[d - 1], trsem.at[d - 1],
                {"lat": lax.rem(lat + d, nlat)},
            )
        )
    for d in range(nlat - 1, 0, -1):

        @pl.when(lat + d < nlat)
        def _():
            sends[d - 1].start()

    lax.fori_loop(second, K, tracer_level, 0)
    os_ref[...] = w[0, c0:c1, 0:C]
    ou_ref[...] = zonal
    ov_ref[...] = w[2, c0:c1, 0:C]
    tot2[...] = jnp.zeros(tot2.shape, F32)
    for d in range(1, nlat):

        @pl.when(lat >= d)
        def _():
            sends[d - 1].wait_recv()
            tot2[...] = tot2[...] + totr[d - 1]

    scale = -1.0 / math.sqrt(R * nlat)
    op_ref[...] = (op_ref[...] + tot2[...]) * scale
    for d in range(1, nlat):

        @pl.when(lat + d < nlat)
        def _():
            sends[d - 1].wait_send()

    for copy in (col_w, col_e, far_w, far_e):
        copy.wait_send()


def hand_over(*refs):
    half = len(refs) // 2
    copies = [
        pltpu.make_async_copy(refs[i], refs[half + i], refs[-1].at[i]) for i in range(half)
    ]
    for copy in copies:
        copy.start()
    for copy in copies:
        copy.wait()


def body(ocean_state, surface_height, zonal_transport, meridional_transport, land_mask, levels):
    nlat, nlon = lax.axis_size("lat"), lax.axis_size("lon")
    _, K, R, C = ocean_state.shape
    wide = (R + 2 * RIM, C + LANES)
    plane = jax.ShapeDtypeStruct((R, C), F32)
    pack = -(-(3 * K + 1) // 8) * 8
    vm = lambda *shape: pltpu.VMEM(shape, F32)
    dma = lambda n: pltpu.SemaphoreType.DMA((n,))
    args = (ocean_state, surface_height, zonal_transport, meridional_transport, land_mask, levels)
    args = [pltpu.with_memory_space_constraint(x, pltpu.HBM) for x in args]
    results = pl.pallas_call(
        functools.partial(kernel, nlat, nlon, K, R, C),
        out_shape=(jax.ShapeDtypeStruct(ocean_state.shape, F32), plane, plane, plane, plane),
        in_specs=[pl.BlockSpec(memory_space=pltpu.HBM)] * 6,
        out_specs=(pl.BlockSpec(memory_space=pltpu.VMEM),) * 5,
        scratch_shapes=[
            vm(2, K, R + 8, C), vm(2, K, R, C), vm(K, R + 8, C),
            pltpu.VMEM((2, R, C), jnp.int32),
            vm(6, *wide), vm(R, C), vm(R, C), vm(R, LANES), vm(2, K, 1, C),
            vm(R, LANES), vm(R, LANES), vm(R, LANES), vm(R, LANES),
            vm(pack, C), vm(pack, C), vm(pack, C), vm(pack, C), vm(pack, C),
            vm(4, RIM, C), vm(2, RIM, C),
            vm(wide[0], LANES), vm(wide[0], LANES), vm(wide[0], LANES), vm(wide[0], LANES),
            vm(*wide), vm(*wide), vm(RIM, wide[1]), vm(RIM, wide[1]),
            vm(1, C), vm(1, C), vm(nlat - 1, 1, C),
            dma(7), dma(10), dma(10), dma(nlat - 1), dma(nlat - 1),
        ],
        compiler_params=pltpu.CompilerParams(
            collective_id=0, has_side_effects=True, vmem_limit_bytes=40 * 1024 * 1024
        ),
        cost_estimate=pl.CostEstimate(
            flops=40_000_000, bytes_accessed=2 * ocean_state.size * 4, transcendentals=0
        ),
    )(*args)
    return pl.pallas_call(
        hand_over,
        out_shape=tuple(pltpu.HBM(x.shape, x.dtype) for x in results),
        in_specs=[pl.BlockSpec(memory_space=pltpu.VMEM)] * 5,
        out_specs=(pl.BlockSpec(memory_space=pltpu.HBM),) * 5,
        scratch_shapes=[dma(5)],
        compiler_params=pltpu.CompilerParams(vmem_limit_bytes=4 * 1024 * 1024),
    )(*[pltpu.with_memory_space_constraint(x, pltpu.VMEM) for x in results])


def solution(mesh):
    cells = P("lat", "lon")
    full = P(None, None, "lat", "lon")
    return jax.shard_map(
        body,
        mesh=mesh,
        in_specs=(full, cells, cells, cells, cells, cells),
        out_specs=(full, cells, cells, cells, cells),
        check_vma=False,
    )
```

```python
import functools
import math

import jax
import jax.numpy as jnp
from jax import lax
from jax.experimental import pallas as pl
from jax.experimental.pallas import tpu as pltpu
from jax.sharding import PartitionSpec as P

NSUB = 10
RIM = 16
CH = 16
LANES = 128
F32 = jnp.float32
MESH = pl.DeviceIdType.MESH


def iota(shape, dim):
    return lax.broadcasted_iota(jnp.int32, shape, dim)


def exact_dot(a, b):
    return jnp.dot(a, b, precision=lax.Precision.HIGHEST, preferred_element_type=F32)


def anti(size):
    return (iota((size, size), 0) + iota((size, size), 1) == size - 1).astype(F32)


def anti_blocks(size, block):
    a, b = iota((size, size), 0), iota((size, size), 1)
    same = (a // block) == (b // block)
    return (same & (a % block + b % block == block - 1)).astype(F32)


def remote(src, dst, send, recv, where):
    return pltpu.make_async_remote_copy(
        src_ref=src, dst_ref=dst, send_sem=send, recv_sem=recv, device_id=where, device_id_type=MESH
    )


def kernel(
    nlat, nlon, K, R, C,
    st_hbm, s_hbm, u_hbm, v_hbm, mask_hbm, lev_hbm,
    ns, os_ref, ou_ref, ov_ref, op_ref,
    ts, uv, pr, ml, w, le, ln, fw0, fs0,
    pcw, pce, re, rw, pkn, pks, rn, rs, fold1, fold4, foldf,
    c2w, c2e, r2e, r2w, ae, an, dd, gg, tot, tot2, totr,
    lsem, ssem, rsem, tssem, trsem,
):
    lat, lon = lax.axis_index("lat"), lax.axis_index("lon")
    east, west = lax.rem(lon + 1, nlon), lax.rem(lon + nlon - 1, nlon)
    up, down = lax.rem(lat + 1, nlat), lax.rem(lat + nlat - 1, nlat)
    is_top, is_low = lat == nlat - 1, lat == 0
    not_top, not_low = lat < nlat - 1, lat > 0
    turned = nlon - 1 - lon
    W = C + LANES
    c0, c1 = RIM, RIM + R
    last = C - LANES

    barrier = pltpu.get_barrier_semaphore()
    for d in range(1, nlon):
        pl.semaphore_signal(
            barrier, inc=1, device_id={"lon": lax.rem(lon + d, nlon)}, device_id_type=MESH
        )
    for d in range(1, nlat):
        pl.semaphore_signal(
            barrier, inc=1, device_id={"lat": lax.rem(lat + d, nlat)}, device_id_type=MESH
        )

    loads = [
        pltpu.make_async_copy(mask_hbm, ml.at[0], lsem.at[0]),
        pltpu.make_async_copy(lev_hbm, ml.at[1], lsem.at[1]),
        pltpu.make_async_copy(st_hbm.at[0:2], ts.at[:, :, 0:R, :], lsem.at[2]),
        pltpu.make_async_copy(st_hbm.at[2:4], uv, lsem.at[3]),
        pltpu.make_async_copy(s_hbm, w.at[0, c0:c1, 0:C], lsem.at[4]),
        pltpu.make_async_copy(u_hbm, w.at[1, c0:c1, 0:C], lsem.at[5]),
        pltpu.make_async_copy(v_hbm, w.at[2, c0:c1, 0:C], lsem.at[6]),
    ]
    for load in loads:
        load.start()

    col_w = remote(pcw, re, ssem.at[0], rsem.at[0], {"lon": west})
    col_e = remote(pce, rw, ssem.at[1], rsem.at[1], {"lon": east})
    row_n = remote(pkn, rs, ssem.at[2], rsem.at[2], {"lat": up})
    row_s = remote(pks, rn, ssem.at[3], rsem.at[3], {"lat": down})
    row_f = remote(fold1, rn, ssem.at[2], rsem.at[3], {"lon": turned})
    hi, lo = pl.ds(c1 - RIM, RIM), pl.ds(c0, RIM)
    above, below = pl.ds(c1, RIM), pl.ds(0, RIM)
    cols = pl.ds(0, C)
    four, two = pl.ds(0, 4), pl.ds(4, 2)
    wid_n = remote(w.at[four, hi, cols], w.at[four, below, cols], ssem.at[4], rsem.at[4], {"lat": up})
    wid_s = remote(w.at[four, lo, cols], w.at[four, above, cols], ssem.at[5], rsem.at[5], {"lat": down})
    wid_f = remote(fold4, w.at[four, above, cols], ssem.at[4], rsem.at[5], {"lon": turned})
    frc_n = remote(w.at[two, hi, cols], w.at[two, below, cols], ssem.at[6], rsem.at[6], {"lat": up})
    frc_s = remote(w.at[two, lo, cols], w.at[two, above, cols], ssem.at[7], rsem.at[7], {"lat": down})
    frc_f = remote(foldf, w.at[two, above, cols], ssem.at[6], rsem.at[7], {"lon": turned})
    far_w = remote(c2w, r2e, ssem.at[8], rsem.at[8], {"lon": west})
    far_e = remote(c2e, r2w, ssem.at[9], rsem.at[9], {"lon": east})

    @pl.when(is_low)
    def _():
        w[:, 0:RIM, 0:C] = jnp.zeros((6, RIM, C), F32)
        rs[...] = jnp.zeros(rs.shape, F32)

    dd[...] = jnp.zeros(dd.shape, F32)
    gg[...] = jnp.zeros(gg.shape, F32)

    lane = iota((CH, LANES), 1)
    lane_c = iota((CH, C), 1)
    row_c = iota((CH, C), 0)
    chunks = range(0, R, CH)
    loads[0].wait()
    loads[1].wait()
    for r in chunks:
        level = (ml[0, r : r + CH, :] * ml[1, r : r + CH, :]).astype(F32)
        w[3, c0 + r : c0 + r + CH, 0:C] = level
        l0, l1 = level[:, :LANES], level[:, last:]
        pcw[r : r + CH, :] = jnp.where(lane == 3 * K, pltpu.roll(l0, 3 * K, 1), 0.0)
        pce[r : r + CH, :] = jnp.where(lane == 3 * K, pltpu.roll(l1, 3 * K + 1, 1), 0.0)
    loads[2].wait()
    loads[3].wait()
    per = 2.0 / (K * (K + 1))

    def pressure_level(k, sums):
        kf = k.astype(F32)
        thick = (kf + 1.0) * per
        out = []
        for i, r in enumerate(chunks):
            rr = slice(r, r + CH)
            t, s = ts[0, k, rr, :], ts[1, k, rr, :]
            level = w[3, c0 + r : c0 + r + CH, 0:C]
            weight = jnp.where(kf < level, 0.8 * s - 0.3 * t - 0.04 * t * t, 0.0) * thick
            press = sums[i] + 0.5 * weight
            out.append(sums[i] + weight)
            pr[k, rr, :] = press
            u1 = uv[0, k, rr, last:]
            t0, s0, p0 = t[:, :LANES], s[:, :LANES], press[:, :LANES]
            t1, s1 = t[:, last:], s[:, last:]
            a = pcw[rr, :]
            a = jnp.where(lane == k, pltpu.roll(t0, k, 1), a)
            a = jnp.where(lane == K + k, pltpu.roll(s0, K + k, 1), a)
            a = jnp.where(lane == 2 * K + k, pltpu.roll(p0, 2 * K + k, 1), a)
            pcw[rr, :] = a
            b = pce[rr, :]
            b = jnp.where(lane == k, pltpu.roll(t1, k + 1, 1), b)
            b = jnp.where(lane == K + k, pltpu.roll(s1, K + k + 1, 1), b)
            b = jnp.where(lane == 2 * K + k, pltpu.roll(u1, 2 * K + k + 1, 1), b)
            pce[rr, :] = b
        return tuple(out)

    lax.fori_loop(0, K, pressure_level, tuple(jnp.zeros((CH, C), F32) for _ in chunks), unroll=5)
    for k in range(K):
        pkn[k : k + 1, :] = ts[0, k, R - 1 : R, :]
        pkn[K + k : K + k + 1, :] = ts[1, k, R - 1 : R, :]
        pkn[2 * K + k : 2 * K + k + 1, :] = uv[1, k, R - 1 : R, :]
        pks[k : k + 1, :] = ts[0, k, 0:1, :]
        pks[K + k : K + k + 1, :] = ts[1, k, 0:1, :]
        pks[2 * K + k : 2 * K + k + 1, :] = pr[k, 0:1, :]
    pkn[3 * K : 3 * K + 1, :] = w[3, c1 - 1 : c1, 0:C]
    pks[3 * K : 3 * K + 1, :] = w[3, c0 : c0 + 1, 0:C]

    pl.semaphore_wait(barrier, nlat + nlon - 2)

    @pl.when(is_top)
    def _():
        for k in range(K):
            fold1[k : k + 1, :] = ts[0, k, R - 1 : R, :]
            fold1[K + k : K + k + 1, :] = ts[1, k, R - 1 : R, :]
            fold1[2 * K + k : 2 * K + k + 1, :] = pr[k, R - 1 : R, :]
        fold1[3 * K : 3 * K + 1, :] = w[3, c1 - 1 : c1, 0:C]
        fold1[3 * K + 1 :, :] = jnp.zeros((fold1.shape[0] - 3 * K - 1, C), F32)
        fold1[...] = exact_dot(fold1[...], anti(C))
        row_f.start()

    col_w.start()
    col_e.start()

    @pl.when(not_top)
    def _():
        row_n.start()

    @pl.when(not_low)
    def _():
        row_s.start()

    for load in loads[4:]:
        load.wait()

    @pl.when(not_top)
    def _():
        wid_n.start()

    @pl.when(is_top)
    def _():
        rows4 = jnp.concatenate([w[f, c1 - RIM : c1, 0:C] for f in range(4)], axis=0)
        flipped = exact_dot(exact_dot(anti_blocks(4 * RIM, RIM), rows4), anti(C))
        for f in range(4):
            fold4[f] = flipped[f * RIM : (f + 1) * RIM]
        wid_f.start()

    @pl.when(not_low)
    def _():
        wid_s.start()

    col_w.wait_recv()
    row_s.wait_recv()
    for k in range(K):
        ts[0, k, R : R + 1, :] = rn[k : k + 1, :]
        ts[1, k, R : R + 1, :] = rn[K + k : K + k + 1, :]
        pr[k, R : R + 1, :] = rn[2 * K + k : 2 * K + k + 1, :]

    def eastward(centre, rim, shift):
        rolled = pltpu.roll(centre, C - 1, 1)
        h = pltpu.roll(rim, shift, 1)
        edge = jnp.where(lane == LANES - 1, h, rolled[:, last:])
        return jnp.concatenate([rolled[:, :last], edge], axis=1)

    for r in chunks:
        level = w[3, c0 + r : c0 + r + CH, 0:C]
        le[r : r + CH, :] = jnp.minimum(
            level, eastward(level, re[r : r + CH, :], LANES - 1 - 3 * K)
        )
        if r + CH < R:
            north = w[3, c0 + r + 1 : c0 + r + CH + 1, 0:C]
        else:
            north = jnp.where(
                row_c == CH - 1, rn[3 * K : 3 * K + 1, :], pltpu.roll(level, CH - 1, 0)
            )
        ln[r : r + CH, :] = jnp.minimum(level, north)

    for r in chunks:
        rr = slice(r, r + CH)
        le_r, ln_r, rim = le[rr, :], ln[rr, :], re[rr, :]

        def force_level(k, sums):
            fx, fy = sums
            kf = k.astype(F32)
            thick = (kf + 1.0) * per
            press = pr[k, rr, :]
            p_e = eastward(press, rim, LANES - 1 - 2 * K - k)
            p_n = pr[k, r + 1 : r + CH + 1, :]
            open_e, open_n = kf < le_r, kf < ln_r
            gx = jnp.where(open_e, p_e - press, 0.0)
            gy = jnp.where(open_n, p_n - press, 0.0)
            ns[2, k, rr, :] = jnp.where(open_e, uv[0, k, rr, :] - 0.2 * gx, 0.0)
            ns[3, k, rr, :] = jnp.where(open_n, uv[1, k, rr, :] - 0.2 * gy, 0.0)
            return fx + gx * thick, fy + gy * thick

        zero = jnp.zeros((CH, C), F32)
        fx, fy = lax.fori_loop(0, K, force_level, (zero, zero), unroll=10)
        w[4, c0 + r : c0 + r + CH, 0:C] = 0.1 * fx
        w[5, c0 + r : c0 + r + CH, 0:C] = 0.1 * fy

    @pl.when(not_top)
    def _():
        frc_n.start()

    @pl.when(is_top)
    def _():
        rows2 = jnp.concatenate([w[f, c1 - RIM : c1, 0:C] for f in (4, 5)], axis=0)
        flipped = exact_dot(exact_dot(anti_blocks(2 * RIM, RIM), rows2), anti(C))
        foldf[0] = flipped[:RIM]
        foldf[1] = flipped[RIM:]
        frc_f.start()

    @pl.when(not_low)
    def _():
        frc_s.start()

    col_e.wait_recv()

    @pl.when(not_low)
    def _():
        row_n.wait_recv()

    lane_f = jnp.where(lane < K, lane, lane - K).astype(F32)
    for r in chunks:
        rr = slice(r, r + CH)
        a, b = rw[rr, :], pcw[rr, :]
        u = jnp.where(lane < K, pltpu.roll(a, LANES - 2 * K, 1), pltpu.roll(a, LANES - K, 1))
        shallow = jnp.minimum(a[:, 3 * K : 3 * K + 1], b[:, 3 * K : 3 * K + 1])
        flux = (jnp.maximum(u, 0.0) + 0.1) * a + (jnp.minimum(u, 0.0) - 0.1) * b
        fw0[rr, :] = jnp.where(lane_f < shallow, flux, 0.0)
    row_k = iota((K, C), 0).astype(F32)
    shallow = jnp.minimum(rs[3 * K : 3 * K + 1, :], pks[3 * K : 3 * K + 1, :])
    v_rim = rs[2 * K : 3 * K, :]
    vp, vm = jnp.maximum(v_rim, 0.0) + 0.1, jnp.minimum(v_rim, 0.0) - 0.1
    for q in range(2):
        flux = vp * rs[q * K : (q + 1) * K, :] + vm * pks[q * K : (q + 1) * K, :]
        flux = jnp.where(row_k < shallow, flux, 0.0)
        for k in range(K):
            fs0[q, k] = flux[k : k + 1, :]

    def tracer_level(k, carry):
        kf = k.astype(F32)
        south_row = [fs0[q, k] for q in range(2)]
        for r in chunks:
            rr = slice(r, r + CH)
            u, v = uv[0, k, rr, :], uv[1, k, rr, :]
            u_p, u_m = jnp.maximum(u, 0.0) + 0.1, jnp.minimum(u, 0.0) - 0.1
            v_p, v_m = jnp.maximum(v, 0.0) + 0.1, jnp.minimum(v, 0.0) - 0.1
            wet = kf < w[3, c0 + r : c0 + r + CH, 0:C]
            wet_e, wet_n = kf < le[rr, :], kf < ln[rr, :]
            rim_e, rim_w = re[rr, :], fw0[rr, :]
            for q in range(2):
                c = ts[q, k, rr, :]
                fe = jnp.where(
                    wet_e, u_p * c + u_m * eastward(c, rim_e, LANES - 1 - q * K - k), 0.0
                )
                fn = jnp.where(wet_n, v_p * c + v_m * ts[q, k, r + 1 : r + CH + 1, :], 0.0)
                h = pltpu.roll(rim_w, LANES - q * K - k if q else lax.rem(LANES - k, LANES), 1)
                rolled = pltpu.roll(fe, 1, 1)
                fw = jnp.concatenate(
                    [jnp.where(lane == 0, h, rolled[:, :LANES]), rolled[:, LANES:]], axis=1
                )
                fs = jnp.where(row_c == 0, south_row[q], pltpu.roll(fn, 1, 0))
                south_row[q] = fn[CH - 1 : CH, :]
                ns[q, k, rr, :] = jnp.where(wet, c + 0.2 * (fw - fe + fs - fn), 0.0)
        return carry

    first, second = (4 * K) // 10, (8 * K) // 10
    lax.fori_loop(0, first, tracer_level, 0)

    wid_s.wait_recv()
    frc_s.wait_recv()

    @pl.when(not_low)
    def _():
        wid_n.wait_recv()
        frc_n.wait_recv()

    wide_rows = range(0, R + 2 * RIM, CH)
    for r in wide_rows:
        a = jnp.zeros((CH, LANES), F32)
        b = jnp.zeros((CH, LANES), F32)
        for f in range(6):
            mine = (lane >= f * RIM) & (lane < (f + 1) * RIM)
            x0 = w[f, r : r + CH, 0:LANES]
            x1 = w[f, r : r + CH, last:C]
            a = jnp.where(mine, pltpu.roll(x0, f * RIM, 1) if f else x0, a)
            b = jnp.where(mine, pltpu.roll(x1, (RIM + f * RIM) % LANES, 1), b)
        c2w[r : r + CH, :] = a
        c2e[r : r + CH, :] = b
    far_w.start()
    far_e.start()
    lax.fori_loop(first, second, tracer_level, 0)
    far_w.wait_recv()
    far_e.wait_recv()
    for r in wide_rows:
        a, b = r2e[r : r + CH, :], r2w[r : r + CH, :]
        for f in range(6):
            x = pltpu.roll(a, LANES - f * RIM, 1) if f else a
            y = pltpu.roll(b, (LANES - RIM - f * RIM) % LANES, 1)
            w[f, r : r + CH, C:W] = jnp.where(
                lane < RIM, x, jnp.where(lane >= LANES - RIM, y, 0.0)
            )

    @pl.when(not_top)
    def _():
        row_n.wait_send()
        wid_n.wait_send()
        frc_n.wait_send()

    @pl.when(not_low)
    def _():
        row_s.wait_send()
        wid_s.wait_send()
        frc_s.wait_send()

    lane_w = iota((CH, W), 1)
    row_w = iota((CH, W), 0)

    @pl.when(is_top)
    def _():
        row_f.wait_send()
        wid_f.wait_send()
        frc_f.wait_send()
        fold = slice(c1, c1 + RIM)
        for f in (1, 4):
            w[f, fold, :] = -pltpu.roll(w[f, fold, :], W - 1, 1)
        for f, where in ((2, dd), (5, gg)):
            x = w[f, fold, :]
            where[...] = jnp.where(row_w == 0, w[f, c1 - 1 : c1, :] + x, 0.0)
            w[f, fold, :] = -pltpu.roll(x, RIM - 1, 0)

    def wide_depth(shallow):
        return (shallow * (shallow + 1.0)) * (0.8 / (K * (K + 1)))

    def shifted_rows(ref, f, r, by):
        low = r + by
        if low < 0 or low + CH > R + 2 * RIM:
            return pltpu.roll(ref[f, r : r + CH, :], (-by) % CH, 0)
        return ref[f, low : low + CH, :]

    def surface_step(first_step):
        for r in wide_rows:
            rr = slice(r, r + CH)
            u, v = w[1, rr, :], w[2, rr, :]
            div = u - pltpu.roll(u, 1, 1) + (v - shifted_rows(w, 2, r, -1))
            if r == c1:
                div = div + dd[...]
            new = w[0, rr, :] - 0.5 * div
            if first_step:
                new = jnp.where(w[3, rr, :] > 0.0, new, 0.0)
            w[0, rr, :] = new

    def transport_step(first_step):
        for r in wide_rows:
            rr = slice(r, r + CH)
            s, u, v = w[0, rr, :], w[1, rr, :], w[2, rr, :]
            if first_step:
                level = w[3, rr, :]
                shallow_e = jnp.minimum(level, pltpu.roll(level, W - 1, 1))
                shallow_n = jnp.minimum(level, shifted_rows(w, 3, r, 1))
                ae[rr, :] = wide_depth(shallow_e)
                an[rr, :] = wide_depth(shallow_n)
                u = jnp.where(shallow_e > 0.0, u, 0.0)
                v = jnp.where(shallow_n > 0.0, v, 0.0)
            w[1, rr, :] = u - ae[rr, :] * (pltpu.roll(s, W - 1, 1) - s) - w[4, rr, :]
            w[2, rr, :] = v - an[rr, :] * (shifted_rows(w, 0, r, 1) - s) - w[5, rr, :]

    surface_step(True)
    transport_step(True)
    dd[...] = jnp.where(an[c1 - 1 : c1, :] > 0.0, dd[...], 0.0) - gg[...]

    def substep(i, carry):
        surface_step(False)
        transport_step(False)
        dd[...] = dd[...] - gg[...]
        return carry

    lax.fori_loop(1, NSUB, substep, 0, unroll=3)

    low_tri = (iota((R, R), 0) >= iota((R, R), 1)).astype(F32)
    zonal = w[1, c0:c1, 0:C]
    op_ref[...] = exact_dot(low_tri, zonal)
    tot[...] = op_ref[R - 1 : R, :]
    sends = []
    for d in range(1, nlat):
        sends.append(
            remote(
                tot, totr.at[d - 1], tssem.at[d - 1], trsem.at[d - 1],
                {"lat": lax.rem(lat + d, nlat)},
            )
        )
    for d in range(nlat - 1, 0, -1):

        @pl.when(lat + d < nlat)
        def _():
            sends[d - 1].start()

    lax.fori_loop(second, K, tracer_level, 0)
    os_ref[...] = w[0, c0:c1, 0:C]
    ou_ref[...] = zonal
    ov_ref[...] = w[2, c0:c1, 0:C]
    tot2[...] = jnp.zeros(tot2.shape, F32)
    for d in range(1, nlat):

        @pl.when(lat >= d)
        def _():
            sends[d - 1].wait_recv()
            tot2[...] = tot2[...] + totr[d - 1]

    scale = -1.0 / math.sqrt(R * nlat)
    op_ref[...] = (op_ref[...] + tot2[...]) * scale
    for d in range(1, nlat):

        @pl.when(lat + d < nlat)
        def _():
            sends[d - 1].wait_send()

    for copy in (col_w, col_e, far_w, far_e):
        copy.wait_send()


def hand_over(*refs):
    half = len(refs) // 2
    copies = [
        pltpu.make_async_copy(refs[i], refs[half + i], refs[-1].at[i]) for i in range(half)
    ]
    for copy in copies:
        copy.start()
    for copy in copies:
        copy.wait()


def body(ocean_state, surface_height, zonal_transport, meridional_transport, land_mask, levels):
    nlat, nlon = lax.axis_size("lat"), lax.axis_size("lon")
    _, K, R, C = ocean_state.shape
    wide = (R + 2 * RIM, C + LANES)
    plane = jax.ShapeDtypeStruct((R, C), F32)
    pack = -(-(3 * K + 1) // 8) * 8
    vm = lambda *shape: pltpu.VMEM(shape, F32)
    dma = lambda n: pltpu.SemaphoreType.DMA((n,))
    args = (ocean_state, surface_height, zonal_transport, meridional_transport, land_mask, levels)
    args = [pltpu.with_memory_space_constraint(x, pltpu.HBM) for x in args]
    results = pl.pallas_call(
        functools.partial(kernel, nlat, nlon, K, R, C),
        out_shape=(jax.ShapeDtypeStruct(ocean_state.shape, F32), plane, plane, plane, plane),
        in_specs=[pl.BlockSpec(memory_space=pltpu.HBM)] * 6,
        out_specs=(pl.BlockSpec(memory_space=pltpu.VMEM),) * 5,
        scratch_shapes=[
            vm(2, K, R + 8, C), vm(2, K, R, C), vm(K, R + 8, C),
            pltpu.VMEM((2, R, C), jnp.int32),
            vm(6, *wide), vm(R, C), vm(R, C), vm(R, LANES), vm(2, K, 1, C),
            vm(R, LANES), vm(R, LANES), vm(R, LANES), vm(R, LANES),
            vm(pack, C), vm(pack, C), vm(pack, C), vm(pack, C), vm(pack, C),
            vm(4, RIM, C), vm(2, RIM, C),
            vm(wide[0], LANES), vm(wide[0], LANES), vm(wide[0], LANES), vm(wide[0], LANES),
            vm(*wide), vm(*wide), vm(RIM, wide[1]), vm(RIM, wide[1]),
            vm(1, C), vm(1, C), vm(nlat - 1, 1, C),
            dma(7), dma(10), dma(10), dma(nlat - 1), dma(nlat - 1),
        ],
        compiler_params=pltpu.CompilerParams(
            collective_id=0, has_side_effects=True, vmem_limit_bytes=40 * 1024 * 1024
        ),
        cost_estimate=pl.CostEstimate(
            flops=40_000_000, bytes_accessed=2 * ocean_state.size * 4, transcendentals=0
        ),
    )(*args)
    return pl.pallas_call(
        hand_over,
        out_shape=tuple(pltpu.HBM(x.shape, x.dtype) for x in results),
        in_specs=[pl.BlockSpec(memory_space=pltpu.VMEM)] * 5,
        out_specs=(pl.BlockSpec(memory_space=pltpu.HBM),) * 5,
        scratch_shapes=[dma(5)],
        compiler_params=pltpu.CompilerParams(vmem_limit_bytes=4 * 1024 * 1024),
    )(*[pltpu.with_memory_space_constraint(x, pltpu.VMEM) for x in results])


def solution(mesh):
    cells = P("lat", "lon")
    full = P(None, None, "lat", "lon")
    return jax.shard_map(
        body,
        mesh=mesh,
        in_specs=(full, cells, cells, cells, cells, cells),
        out_specs=(full, cells, cells, cells, cells),
        check_vma=False,
    )
```
